32 devices in a mesh: seq: 8 (over z, x), chan: 4 (over y, core).
Axes of the slice: x: 2, y: 2, z: 4, core: 2. Of those that a mesh axis runs over, the one named last changes fastest.
Arguments:
- inputs: bfloat16 [1024, 2048], P('seq', 'chan'), may hold values from -6 to 6
- gate_branch: bfloat16 [1024, 2048], P('seq', 'chan'), may hold values from -6 to 6
- short_taps: float32 [4, 2048], P(None, 'chan'), may hold values from -3 to 3
- filters: float32 [1024, 2048], P('seq', 'chan'), may hold values from -0.1875 to 0.1875
- w_out: bfloat16 [2048, 2048], P('chan'), may hold values from -0.125 to 0.125
- cotangent: bfloat16 [1024, 2048], P('seq', 'chan'), may hold values from -6 to 6
Outputs:
- output: bfloat16 [1024, 2048], P('seq', 'chan')
- grad_inputs: bfloat16 [1024, 2048], P('seq', 'chan')
- grad_gate: bfloat16 [1024, 2048], P('seq', 'chan')
- grad_filters: float32 [1024, 2048], P('seq', 'chan')
- grad_taps: float32 [4, 2048], P(None, 'chan')
- grad_wout: float32 [2048, 2048], P('chan', 'seq')
The draws below stay inside these ranges and needn't reach their ends.
All inputs are finite; a program needn't handle non-finite values.
Results may differ from the reference program's by a relative error of at most 0.0047.
The reference program's roundings to bfloat16 on the way (of `gated`) count: a program that leaves them out, or rounds other values in their place, can miss the bound.
Values may be sent and summed in bfloat16 or wider, within the bound.
A program may use at most 64 MiB of HBM per device.

```python
import jax
import jax.numpy as jnp

D = 2048
KS = 4
TOKENS = 1024


def raised(entries, key, source, target, parts, factor):
    owner, partner = [(jnp.arange(entries.shape[dim]) // (entries.shape[dim] // parts)).reshape([-1 if axis == dim else 1 for axis in range(entries.ndim)]) for dim in (source, target)]
    chosen = jax.random.permutation(key, parts)[partner]
    strong = (owner == chosen) | (owner == (partner + parts // 2) % parts)
    return jnp.where(strong, factor * entries, entries)


def block_levels(rng, shape, cuts, smallest, largest):
    loudness = 1.0
    for position, blocks in cuts:
        heights = jax.random.uniform(jax.random.fold_in(jax.random.fold_in(rng, 6), position), (blocks,), jnp.float32, smallest / len(cuts), largest / len(cuts))
        loudness = loudness * jnp.repeat(jnp.exp(heights), shape[position] // blocks).reshape((-1,) + (1,) * (len(shape) - 1 - position))
    return loudness


def normal_values(own_key, extent, deviation, most, split=(), kind=jnp.bfloat16):
    loudness = block_levels(own_key, extent, split, -0.22, 0.18) if split else 1.0
    values = jax.random.normal(own_key, extent, jnp.float32) * deviation * loudness
    return jnp.minimum(jnp.maximum(values, -most), most).astype(kind)


def bell_draw_with(own_key, extent, width, bound, shards, heavy, dtype=jnp.bfloat16):
    array = width * jax.random.normal(own_key, extent, jnp.float32)
    if shards:
        array = array * block_levels(own_key, extent, shards, -0.22, 0.18)
    return jnp.clip(raised(array, jax.random.fold_in(own_key, 3), *heavy), -bound, bound).astype(dtype)


def setup_inputs(seed: int = 0) -> dict:
    splits = jax.random.split(jax.random.key(seed), 7)
    inputs = normal_values(splits[0], (TOKENS, D), 1.0, 6.0, ((0, 8), (1, 4)))
    gate_branch = normal_values(splits[1], (TOKENS, D), 1.0, 6.0, ((0, 8), (1, 4)))
    short_taps = normal_values(splits[2], (KS, D), 0.5, 3.0, ((1, 4),), jnp.float32)
    filters = normal_values(splits[3], (TOKENS, D), TOKENS ** -0.5, 0.1875, ((0, 8), (1, 4)), jnp.float32)
    w_out = normal_values(splits[4], (D, D), D ** -0.5, 0.125, ((0, 4),))
    cotangent = bell_draw_with(splits[5], (TOKENS, D), 1.0, 6.0, ((0, 8), (1, 4)), (0, 1, 8, 2.0))
    return dict(inputs=inputs, gate_branch=gate_branch, short_taps=short_taps, filters=filters, w_out=w_out, cotangent=cotangent)


def spectrum(signal):
    padded = jnp.concatenate([signal, jnp.zeros_like(signal)], 0)
    return jnp.fft.rfft(padded, axis=0)


def back_transform(values):
    return jnp.fft.irfft(values, n=2 * TOKENS, axis=0)[:TOKENS].astype(jnp.float32)


def reference(inputs, gate_branch, short_taps, filters, w_out, cotangent):
    widened = inputs.astype(jnp.float32)
    padded = jnp.pad(widened, ((KS - 1, 0), (0, 0)))
    mixed = jnp.zeros_like(widened)
    for tap_index in range(KS):
        mixed = mixed + short_taps[tap_index] * padded[KS - 1 - tap_index:KS - 1 - tap_index + TOKENS]
    mixed_spec = spectrum(mixed)
    filter_spec = spectrum(filters)
    convolved = back_transform(mixed_spec * filter_spec)
    gate_wide = gate_branch.astype(jnp.float32)
    gated = (gate_wide * convolved).astype(jnp.bfloat16)
    output = jnp.dot(gated, w_out, preferred_element_type=jnp.float32).astype(jnp.bfloat16)
    grad_gated = jnp.dot(cotangent, w_out.T, preferred_element_type=jnp.float32)
    grad_gate = (grad_gated * convolved).astype(jnp.bfloat16)
    grad_conv = grad_gated * gate_wide
    grad_spec = spectrum(grad_conv)
    grad_mixed = back_transform(jnp.conj(filter_spec) * grad_spec)
    grad_filters = back_transform(jnp.conj(mixed_spec) * grad_spec)
    grad_padded = jnp.pad(grad_mixed, ((0, KS - 1), (0, 0)))
    grad_wide = jnp.zeros_like(widened)
    tap_rows = []
    for tap_index in range(KS):
        grad_wide = grad_wide + short_taps[tap_index] * grad_padded[tap_index:tap_index + TOKENS]
        shifted = padded[KS - 1 - tap_index:KS - 1 - tap_index + TOKENS]
        tap_rows.append(jnp.sum(shifted * grad_mixed, axis=0))
    grad_inputs = grad_wide.astype(jnp.bfloat16)
    grad_taps = jnp.stack(tap_rows, 0)
    grad_wout = jnp.dot(gated.T, cotangent, preferred_element_type=jnp.float32)
    return output, grad_inputs, grad_gate, grad_filters, grad_taps, grad_wout
```

```python
import math

import jax
import jax.numpy as jnp
import numpy as np
from jax import lax
from jax.sharding import PartitionSpec as P

HIGHEST = lax.Precision.HIGHEST


def from_behind(value, axis, steps):
    count = lax.axis_size(axis)
    first, last = (max(0, -steps), min(count, count - steps))
    return lax.ppermute(value, axis, [(source, source + steps) for source in range(first, last)])


def angle_table(row_len, col_len, modulus, row_start, col_start, direction):
    row_ids = lax.iota(jnp.int32, row_len)[:, None] + row_start
    col_ids = lax.iota(jnp.int32, col_len)[None, :] + col_start
    phase = row_ids * col_ids % modulus
    angles = phase.astype(jnp.float32) * (direction * 2.0 * math.pi / modulus)
    return (jnp.cos(angles), jnp.sin(angles))


def column_dft(real_part, imag_part, length, form, direction):
    cos_table, sin_table = angle_table(length, length, length, 0, 0, direction)
    new_real = jnp.einsum(form, real_part, cos_table, precision=HIGHEST) - jnp.einsum(
        form, imag_part, sin_table, precision=HIGHEST
    )
    new_imag = jnp.einsum(form, real_part, sin_table, precision=HIGHEST) + jnp.einsum(
        form, imag_part, cos_table, precision=HIGHEST
    )
    return (new_real, new_imag)


def panel_forward(signal):
    stack_size = signal.shape[0]
    block_len = signal.shape[1]
    part_count = lax.axis_size("seq")
    my_index = lax.axis_index("seq")
    narrow = block_len // part_count
    row_order = 2 * part_count
    full_len = row_order * block_len
    by_column = lax.all_to_all(signal[:, None], "seq", split_axis=2, concat_axis=1, tiled=True)
    row_cos, row_sin = angle_table(row_order, part_count, row_order, 0, 0, -1.0)
    real_part = jnp.einsum("ja,kabf->kjbf", row_cos, by_column, precision=HIGHEST)
    imag_part = jnp.einsum("ja,kabf->kjbf", row_sin, by_column, precision=HIGHEST)
    twist_cos, twist_sin = angle_table(row_order, narrow, full_len, 0, my_index * narrow, -1.0)
    twist_cos = twist_cos[None, :, :, None]
    twist_sin = twist_sin[None, :, :, None]
    real_twist = real_part * twist_cos - imag_part * twist_sin
    imag_twist = real_part * twist_sin + imag_part * twist_cos
    by_rows = lax.all_to_all(
        jnp.concatenate([real_twist, imag_twist], 0), "seq", split_axis=1, concat_axis=2, tiled=True
    )
    return column_dft(by_rows[:stack_size], by_rows[stack_size:], block_len, "kjbf,bm->kjmf", -1.0)


def panel_inverse(real_part, imag_part):
    stack_size = real_part.shape[0]
    block_len = real_part.shape[2]
    part_count = lax.axis_size("seq")
    my_index = lax.axis_index("seq")
    row_order = 2 * part_count
    full_len = row_order * block_len
    real_back, imag_back = column_dft(real_part, imag_part, block_len, "kjmf,mb->kjbf", 1.0)
    twist_cos, twist_sin = angle_table(2, block_len, full_len, my_index * 2, 0, 1.0)
    twist_cos = twist_cos[None, :, :, None]
    twist_sin = twist_sin[None, :, :, None]
    real_twist = (real_back * twist_cos - imag_back * twist_sin) / block_len
    imag_twist = (real_back * twist_sin + imag_back * twist_cos) / block_len
    by_column = lax.all_to_all(
        jnp.concatenate([real_twist, imag_twist], 0), "seq", split_axis=2, concat_axis=1, tiled=True
    )
    row_cos, row_sin = angle_table(part_count, row_order, row_order, 0, 0, 1.0)
    signal = (
        jnp.einsum("aj,kjbf->kabf", row_cos, by_column[:stack_size], precision=HIGHEST)
        - jnp.einsum("aj,kjbf->kabf", row_sin, by_column[stack_size:], precision=HIGHEST)
    ) / row_order
    returned = lax.all_to_all(signal, "seq", split_axis=1, concat_axis=2, tiled=True)
    return returned[:, 0]


def panel_local(inputs, gate_branch, short_taps, filters, w_out, cotangent):
    forward_fn, inverse_fn = (panel_forward, panel_inverse)
    tap_count = short_taps.shape[0]
    row_count = inputs.shape[0]
    left_tail = from_behind(inputs[row_count - (tap_count - 1) :], "seq", 1)
    extended = jnp.concatenate([left_tail, inputs], 0).astype(jnp.float32)
    mixed = jnp.zeros((row_count, inputs.shape[1]), jnp.float32)
    for tap_index in range(tap_count):
        start_row = tap_count - 1 - tap_index
        mixed = mixed + short_taps[tap_index] * extended[start_row : start_row + row_count]
    spec_real, spec_imag = forward_fn(jnp.stack([mixed, filters], 0))
    mixed_real, filter_real = (spec_real[0], spec_real[1])
    mixed_imag, filter_imag = (spec_imag[0], spec_imag[1])
    prod_real = mixed_real * filter_real - mixed_imag * filter_imag
    prod_imag = mixed_real * filter_imag + mixed_imag * filter_real
    convolved = inverse_fn(prod_real[None], prod_imag[None])[0]
    gate_wide = gate_branch.astype(jnp.float32)
    gated = (gate_wide * convolved).astype(jnp.bfloat16)
    out_terms = jnp.dot(gated, w_out, preferred_element_type=jnp.float32)
    output = lax.psum_scatter(out_terms, "chan", scatter_dimension=1, tiled=True).astype(
        jnp.bfloat16
    )
    full_cot = lax.all_gather(cotangent, "chan", axis=1, tiled=True)
    grad_gated = lax.dot_general(
        full_cot, w_out, (((1,), (1,)), ((), ())), preferred_element_type=jnp.float32
    )
    grad_gate = (grad_gated * convolved).astype(jnp.bfloat16)
    grad_conv = grad_gated * gate_wide
    grad_real, grad_imag = forward_fn(grad_conv[None])
    grad_real = grad_real[0]
    grad_imag = grad_imag[0]
    back_real = jnp.stack(
        [
            filter_real * grad_real + filter_imag * grad_imag,
            mixed_real * grad_real + mixed_imag * grad_imag,
        ],
        0,
    )
    back_imag = jnp.stack(
        [
            filter_real * grad_imag - filter_imag * grad_real,
            mixed_real * grad_imag - mixed_imag * grad_real,
        ],
        0,
    )
    gradients = inverse_fn(back_real, back_imag)
    grad_mixed = gradients[0]
    grad_filters = gradients[1]
    right_head = from_behind(grad_mixed[: tap_count - 1], "seq", -1)
    grad_ext = jnp.concatenate([grad_mixed, right_head], 0)
    grad_wide = jnp.zeros_like(grad_mixed)
    tap_rows = []
    for tap_index in range(tap_count):
        start_row = tap_count - 1 - tap_index
        grad_wide = grad_wide + short_taps[tap_index] * grad_ext[tap_index : tap_index + row_count]
        tap_rows.append(jnp.sum(extended[start_row : start_row + row_count] * grad_mixed, axis=0))
    grad_inputs = grad_wide.astype(jnp.bfloat16)
    grad_taps = lax.psum(jnp.stack(tap_rows, 0), "seq")
    weight_terms = lax.dot_general(
        gated, full_cot, (((0,), (0,)), ((), ())), preferred_element_type=jnp.float32
    )
    grad_wout = lax.psum_scatter(weight_terms, "seq", scatter_dimension=1, tiled=True)
    return (output, grad_inputs, grad_gate, grad_filters, grad_taps, grad_wout)


DENSE_TOKENS = 2048


def split_table(table):
    high = table.astype(jnp.bfloat16)
    low = (table - high.astype(np.float64)).astype(jnp.bfloat16)
    return (high, low)


def dense_tables(tokens):
    freq = np.arange(tokens, dtype=np.int64)[:, None]
    time = np.arange(tokens, dtype=np.int64)[None, :]
    angles = ((2 * freq + 1) * time % (4 * tokens)) * (2.0 * np.pi / (4 * tokens))
    forward = np.concatenate([np.cos(angles), -np.sin(angles)], 0)
    inverse = forward.T / tokens
    return (split_table(forward), split_table(inverse))


def split_value(value):
    rounded = lax.reduce_precision(value, 8, 7)
    return (rounded.astype(jnp.bfloat16), (value - rounded).astype(jnp.bfloat16))


def table_dot(table, value):
    table_high, table_low = table
    high, low = split_value(value)
    width = value.shape[1]
    wide = jnp.dot(
        table_high, jnp.concatenate([high, low], 1), preferred_element_type=jnp.float32
    )
    narrow = jnp.dot(table_low, high, preferred_element_type=jnp.float32)
    return wide[:, :width] + wide[:, width:] + narrow


def shifted_down(value, steps):
    return jnp.pad(value, ((steps, 0), (0, 0)))[: value.shape[0]] if steps else value


def shifted_up(value, steps):
    return jnp.pad(value, ((0, steps), (0, 0)))[steps:] if steps else value


def swap(value, axis):
    return lax.all_to_all(value, axis, split_axis=0, concat_axis=0, tiled=True)


def by_part(value, parts):
    rows, cols = value.shape
    return value.reshape(rows, parts, cols // parts).transpose(1, 0, 2)


def dense_local(inputs, gate_branch, short_taps, filters, w_out, cotangent):
    bf16 = jnp.bfloat16
    f32 = jnp.float32
    parts = lax.axis_size("seq")
    chans = lax.axis_size("chan")
    me = lax.axis_index("seq")
    tap_count = short_taps.shape[0]
    rows, cols = inputs.shape
    narrow = cols // parts
    tokens = rows * parts
    width = cols * chans
    forward, inverse = dense_tables(tokens)

    first = jnp.concatenate([by_part(inputs, parts), by_part(filters.astype(bf16), parts)], 2)
    first = swap(first, "seq").reshape(tokens, 2 * narrow).astype(f32)
    full_cot = lax.all_gather(cotangent, "chan", axis=1, tiled=True)
    grad_gated = lax.dot_general(
        full_cot, w_out, (((1,), (1,)), ((), ())), preferred_element_type=f32
    )
    second = jnp.concatenate(
        [by_part(gate_branch, parts), by_part(grad_gated.astype(bf16), parts)], 2
    )
    second = swap(second, "seq").reshape(tokens, 2 * narrow).astype(f32)

    own_taps = lax.dynamic_slice(short_taps, (0, me * narrow), (tap_count, narrow))
    still = (lax.iota(jnp.int32, tap_count) == 0).astype(f32)[:, None]
    weights = jnp.concatenate([own_taps, jnp.broadcast_to(still, own_taps.shape)], 1)
    mixed = jnp.zeros_like(first)
    for tap in range(tap_count):
        mixed = mixed + weights[tap] * shifted_down(first, tap)
    spec = table_dot(forward, mixed)
    spec_real, spec_imag = (spec[:tokens], spec[tokens:])
    mixed_real, filter_real = (spec_real[:, :narrow], spec_real[:, narrow:])
    mixed_imag, filter_imag = (spec_imag[:, :narrow], spec_imag[:, narrow:])
    product = jnp.concatenate(
        [
            mixed_real * filter_real - mixed_imag * filter_imag,
            mixed_real * filter_imag + mixed_imag * filter_real,
        ],
        0,
    )
    convolved = table_dot(inverse, product)
    gate_wide, gated_wide = (second[:, :narrow], second[:, narrow:])
    gated = (gate_wide * convolved).astype(bf16)
    grad_gate = (gated_wide * convolved).astype(bf16)
    grad_spec = table_dot(forward, gate_wide * gated_wide)
    grad_real, grad_imag = (grad_spec[:tokens], grad_spec[tokens:])
    grad_real = jnp.concatenate([grad_real, grad_real], 1)
    grad_imag = jnp.concatenate([grad_imag, grad_imag], 1)
    swap_real = jnp.concatenate([filter_real, mixed_real], 1)
    swap_imag = jnp.concatenate([filter_imag, mixed_imag], 1)
    back = jnp.concatenate(
        [
            swap_real * grad_real + swap_imag * grad_imag,
            swap_real * grad_imag - swap_imag * grad_real,
        ],
        0,
    )
    gradients = table_dot(inverse, back)
    grad_mixed = gradients[:, :narrow]
    grad_wide = jnp.zeros_like(grad_mixed)
    tap_rows = []
    for tap in range(tap_count):
        grad_wide = grad_wide + own_taps[tap] * shifted_up(grad_mixed, tap)
        tap_rows.append(jnp.sum(shifted_down(first[:, :narrow], tap) * grad_mixed, axis=0))
    grad_taps = lax.all_gather(jnp.stack(tap_rows, 0), "seq", axis=1, tiled=True)

    gated_all = lax.all_gather(gated, "seq", axis=0)
    cot_cols = swap(by_part(full_cot, parts), "seq").reshape(tokens, width // parts)
    own_gated = lax.dynamic_slice(gated_all, (0, me * rows, 0), (parts, rows, narrow))
    own_gated = own_gated.transpose(1, 0, 2).reshape(rows, cols)
    out_terms = jnp.dot(own_gated, w_out, preferred_element_type=f32).astype(bf16)
    out_terms = swap(by_part(out_terms, chans), "chan").astype(f32)
    output = jnp.sum(out_terms, axis=0).astype(bf16)
    grad_wout = lax.dot_general(
        gated_all, cot_cols, (((1,), (0,)), ((), ())), preferred_element_type=f32
    ).reshape(cols, width // parts)

    third = jnp.concatenate(
        [grad_gate, grad_wide.astype(bf16), gradients[:, narrow:].astype(bf16)], 1
    )
    third = swap(third.reshape(parts, rows, 3 * narrow), "seq").transpose(1, 0, 2)
    grad_gate, grad_inputs, grad_filters = (
        third[:, :, index * narrow : (index + 1) * narrow].reshape(rows, cols)
        for index in range(3)
    )
    return (output, grad_inputs, grad_gate, grad_filters.astype(f32), grad_taps, grad_wout)


def local(inputs, *others):
    tokens = inputs.shape[0] * lax.axis_size("seq")
    chosen = dense_local if tokens <= DENSE_TOKENS else panel_local
    return chosen(inputs, *others)


def solution(mesh):
    in_specs = (
        P("seq", "chan"),
        P("seq", "chan"),
        P(None, "chan"),
        P("seq", "chan"),
        P("chan", None),
        P("seq", "chan"),
    )
    out_specs = (
        P("seq", "chan"),
        P("seq", "chan"),
        P("seq", "chan"),
        P("seq", "chan"),
        P(None, "chan"),
        P("chan", "seq"),
    )
    return jax.shard_map(local, mesh=mesh, in_specs=in_specs, out_specs=out_specs, check_vma=False)
```

```python
import math

import functools

import jax
import jax.numpy as jnp
import numpy as np
from jax import lax
from jax.experimental import pallas as pl
from jax.experimental.pallas import tpu as pltpu
from jax.sharding import PartitionSpec as P

HIGHEST = lax.Precision.HIGHEST


def from_behind(value, axis, steps):
    count = lax.axis_size(axis)
    first, last = (max(0, -steps), min(count, count - steps))
    return lax.ppermute(value, axis, [(source, source + steps) for source in range(first, last)])


def angle_table(row_len, col_len, modulus, row_start, col_start, direction):
    row_ids = lax.iota(jnp.int32, row_len)[:, None] + row_start
    col_ids = lax.iota(jnp.int32, col_len)[None, :] + col_start
    phase = row_ids * col_ids % modulus
    angles = phase.astype(jnp.float32) * (direction * 2.0 * math.pi / modulus)
    return (jnp.cos(angles), jnp.sin(angles))


def column_dft(real_part, imag_part, length, form, direction):
    cos_table, sin_table = angle_table(length, length, length, 0, 0, direction)
    new_real = jnp.einsum(form, real_part, cos_table, precision=HIGHEST) - jnp.einsum(
        form, imag_part, sin_table, precision=HIGHEST
    )
    new_imag = jnp.einsum(form, real_part, sin_table, precision=HIGHEST) + jnp.einsum(
        form, imag_part, cos_table, precision=HIGHEST
    )
    return (new_real, new_imag)


def panel_forward(signal):
    stack_size = signal.shape[0]
    block_len = signal.shape[1]
    part_count = lax.axis_size("seq")
    my_index = lax.axis_index("seq")
    narrow = block_len // part_count
    row_order = 2 * part_count
    full_len = row_order * block_len
    by_column = lax.all_to_all(signal[:, None], "seq", split_axis=2, concat_axis=1, tiled=True)
    row_cos, row_sin = angle_table(row_order, part_count, row_order, 0, 0, -1.0)
    real_part = jnp.einsum("ja,kabf->kjbf", row_cos, by_column, precision=HIGHEST)
    imag_part = jnp.einsum("ja,kabf->kjbf", row_sin, by_column, precision=HIGHEST)
    twist_cos, twist_sin = angle_table(row_order, narrow, full_len, 0, my_index * narrow, -1.0)
    twist_cos = twist_cos[None, :, :, None]
    twist_sin = twist_sin[None, :, :, None]
    real_twist = real_part * twist_cos - imag_part * twist_sin
    imag_twist = real_part * twist_sin + imag_part * twist_cos
    by_rows = lax.all_to_all(
        jnp.concatenate([real_twist, imag_twist], 0), "seq", split_axis=1, concat_axis=2, tiled=True
    )
    return column_dft(by_rows[:stack_size], by_rows[stack_size:], block_len, "kjbf,bm->kjmf", -1.0)


def panel_inverse(real_part, imag_part):
    stack_size = real_part.shape[0]
    block_len = real_part.shape[2]
    part_count = lax.axis_size("seq")
    my_index = lax.axis_index("seq")
    row_order = 2 * part_count
    full_len = row_order * block_len
    real_back, imag_back = column_dft(real_part, imag_part, block_len, "kjmf,mb->kjbf", 1.0)
    twist_cos, twist_sin = angle_table(2, block_len, full_len, my_index * 2, 0, 1.0)
    twist_cos = twist_cos[None, :, :, None]
    twist_sin = twist_sin[None, :, :, None]
    real_twist = (real_back * twist_cos - imag_back * twist_sin) / block_len
    imag_twist = (real_back * twist_sin + imag_back * twist_cos) / block_len
    by_column = lax.all_to_all(
        jnp.concatenate([real_twist, imag_twist], 0), "seq", split_axis=2, concat_axis=1, tiled=True
    )
    row_cos, row_sin = angle_table(part_count, row_order, row_order, 0, 0, 1.0)
    signal = (
        jnp.einsum("aj,kjbf->kabf", row_cos, by_column[:stack_size], precision=HIGHEST)
        - jnp.einsum("aj,kjbf->kabf", row_sin, by_column[stack_size:], precision=HIGHEST)
    ) / row_order
    returned = lax.all_to_all(signal, "seq", split_axis=1, concat_axis=2, tiled=True)
    return returned[:, 0]


def panel_local(inputs, gate_branch, short_taps, filters, w_out, cotangent):
    forward_fn, inverse_fn = (panel_forward, panel_inverse)
    tap_count = short_taps.shape[0]
    row_count = inputs.shape[0]
    left_tail = from_behind(inputs[row_count - (tap_count - 1) :], "seq", 1)
    extended = jnp.concatenate([left_tail, inputs], 0).astype(jnp.float32)
    mixed = jnp.zeros((row_count, inputs.shape[1]), jnp.float32)
    for tap_index in range(tap_count):
        start_row = tap_count - 1 - tap_index
        mixed = mixed + short_taps[tap_index] * extended[start_row : start_row + row_count]
    spec_real, spec_imag = forward_fn(jnp.stack([mixed, filters], 0))
    mixed_real, filter_real = (spec_real[0], spec_real[1])
    mixed_imag, filter_imag = (spec_imag[0], spec_imag[1])
    prod_real = mixed_real * filter_real - mixed_imag * filter_imag
    prod_imag = mixed_real * filter_imag + mixed_imag * filter_real
    convolved = inverse_fn(prod_real[None], prod_imag[None])[0]
    gate_wide = gate_branch.astype(jnp.float32)
    gated = (gate_wide * convolved).astype(jnp.bfloat16)
    out_terms = jnp.dot(gated, w_out, preferred_element_type=jnp.float32)
    output = lax.psum_scatter(out_terms, "chan", scatter_dimension=1, tiled=True).astype(
        jnp.bfloat16
    )
    full_cot = lax.all_gather(cotangent, "chan", axis=1, tiled=True)
    grad_gated = lax.dot_general(
        full_cot, w_out, (((1,), (1,)), ((), ())), preferred_element_type=jnp.float32
    )
    grad_gate = (grad_gated * convolved).astype(jnp.bfloat16)
    grad_conv = grad_gated * gate_wide
    grad_real, grad_imag = forward_fn(grad_conv[None])
    grad_real = grad_real[0]
    grad_imag = grad_imag[0]
    back_real = jnp.stack(
        [
            filter_real * grad_real + filter_imag * grad_imag,
            mixed_real * grad_real + mixed_imag * grad_imag,
        ],
        0,
    )
    back_imag = jnp.stack(
        [
            filter_real * grad_imag - filter_imag * grad_real,
            mixed_real * grad_imag - mixed_imag * grad_real,
        ],
        0,
    )
    gradients = inverse_fn(back_real, back_imag)
    grad_mixed = gradients[0]
    grad_filters = gradients[1]
    right_head = from_behind(grad_mixed[: tap_count - 1], "seq", -1)
    grad_ext = jnp.concatenate([grad_mixed, right_head], 0)
    grad_wide = jnp.zeros_like(grad_mixed)
    tap_rows = []
    for tap_index in range(tap_count):
        start_row = tap_count - 1 - tap_index
        grad_wide = grad_wide + short_taps[tap_index] * grad_ext[tap_index : tap_index + row_count]
        tap_rows.append(jnp.sum(extended[start_row : start_row + row_count] * grad_mixed, axis=0))
    grad_inputs = grad_wide.astype(jnp.bfloat16)
    grad_taps = lax.psum(jnp.stack(tap_rows, 0), "seq")
    weight_terms = lax.dot_general(
        gated, full_cot, (((0,), (0,)), ((), ())), preferred_element_type=jnp.float32
    )
    grad_wout = lax.psum_scatter(weight_terms, "seq", scatter_dimension=1, tiled=True)
    return (output, grad_inputs, grad_gate, grad_filters, grad_taps, grad_wout)


DENSE_TOKENS = 2048


def split_table(table):
    high = table.astype(jnp.bfloat16)
    low = (table - high.astype(np.float64)).astype(jnp.bfloat16)
    return (high, low)


def dense_tables(tokens):
    freq = np.arange(tokens, dtype=np.int64)[:, None]
    time = np.arange(tokens, dtype=np.int64)[None, :]
    angles = ((2 * freq + 1) * time % (4 * tokens)) * (2.0 * np.pi / (4 * tokens))
    forward = np.concatenate([np.cos(angles), -np.sin(angles)], 0)
    inverse = forward.T / tokens
    return (split_table(forward), split_table(inverse))


LANES = 128
HALF = 64
TILE = 256
BF16 = jnp.bfloat16
F32 = jnp.float32


def left_half(shape):
    return lax.broadcasted_iota(jnp.int32, shape, 1) < HALF


def turned(value):
    return pltpu.roll(value, HALF, 1)


def split_value(value):
    high = value.astype(BF16)
    return (high, (value - high.astype(F32)).astype(BF16))


def packed_split(value):
    high = value.astype(BF16).astype(F32)
    return jnp.where(left_half(value.shape), high, value - high).astype(BF16)


def tiles(count, body):
    def step(index, carry):
        body(pl.ds(pl.multiple_of(index * TILE, TILE), TILE))
        return carry

    lax.fori_loop(0, count // TILE, step, 0)


def product(left, right):
    return jnp.dot(left, right, preferred_element_type=F32)


def wide_transform(high, low, value, result):
    def body(rows):
        first = product(high[rows, :], value[...])
        second = product(low[rows, :], value[:, :LANES])
        result[rows, :] = first[:, :LANES] + first[:, LANES:] + second

    tiles(result.shape[0], body)


def half_transform(high, low, value, result):
    def body(rows):
        total = product(high[rows, :], value[...]) + product(low[rows, :], value[...])
        result[rows, :] = total + turned(total)

    tiles(result.shape[0], body)


def moved(value, steps):
    if steps == 0:
        return value
    count = value.shape[0]
    row = lax.broadcasted_iota(jnp.int32, value.shape, 0)
    keep = (row >= steps) if steps > 0 else (row < count + steps)
    return jnp.where(keep, pltpu.roll(value, steps % count, 0), 0.0)


def block_kernel(
    inputs, gate, taps, filters, w_out, cot, fwd_high_hbm, fwd_low_hbm, inv_high_hbm, inv_low_hbm,
    output, grad_inputs, grad_gate, grad_filters, grad_taps, grad_wout,
    fwd_high, fwd_low, inv_high, inv_low, cot_all, cot_send, cot_cols, first_send, first_got,
    second_send, second_got, gated_all, third_send, third_got, gate_send, gate_got,
    taps_send, taps_got, part_send, part_got, wide_short, half_short, half_long, wide_long,
    spec, grad_spec, signal, mixing, table_sems, send_sems, recv_sems, chan_send_sems, chan_recv_sems,
):
    parts, rows = first_got.shape[0], first_got.shape[1]
    chans, cols = cot_all.shape[0], inputs.shape[1]
    tokens = parts * rows
    tap_count = taps.shape[0]
    me = lax.axis_index("seq")
    mine = lax.axis_index("chan")

    tables = [
        pltpu.make_async_copy(source, target, table_sems.at[index])
        for index, (source, target) in enumerate(
            [
                (fwd_high_hbm, fwd_high), (fwd_low_hbm, fwd_low),
                (inv_high_hbm, inv_high), (inv_low_hbm, inv_low),
            ]
        )
    ]
    for table in tables:
        table.start()

    barrier = pltpu.get_barrier_semaphore()
    for step in range(1, parts):
        pl.semaphore_signal(
            barrier, inc=1, device_id=(lax.rem(me + step, parts), mine),
            device_id_type=pl.DeviceIdType.MESH,
        )
    for step in range(1, chans):
        pl.semaphore_signal(
            barrier, inc=1, device_id=(me, lax.rem(mine + step, chans)),
            device_id_type=pl.DeviceIdType.MESH,
        )
    pl.semaphore_wait(barrier, parts + chans - 2)

    def to_seq(kind, step, source, target):
        return pltpu.make_async_remote_copy(
            src_ref=source, dst_ref=target,
            send_sem=send_sems.at[kind, step], recv_sem=recv_sems.at[kind, step],
            device_id=(lax.rem(me + step, parts), mine), device_id_type=pl.DeviceIdType.MESH,
        )

    def to_chan(kind, step, source, target):
        return pltpu.make_async_remote_copy(
            src_ref=source, dst_ref=target,
            send_sem=chan_send_sems.at[kind, step], recv_sem=chan_recv_sems.at[kind, step],
            device_id=(me, lax.rem(mine + step, chans)), device_id_type=pl.DeviceIdType.MESH,
        )

    def launch(copies):
        for copy in copies:
            copy.start()
        return copies

    def arrive(copies):
        for copy in copies:
            copy.wait_recv()

    def exchange(kind, sent, got):
        copies = launch(
            [
                to_seq(kind, step, sent.at[lax.rem(me + step, parts)], got.at[me])
                for step in range(1, parts)
            ]
        )
        got[pl.ds(me, 1)] = sent[pl.ds(me, 1)]
        return copies

    def pack(left, right, target):
        for pair in range(parts // 2):
            span = slice(pair * LANES, (pair + 1) * LANES)
            a, b = (left[:, span].astype(F32), right[:, span].astype(F32))
            low = left_half(a.shape)
            target[2 * pair] = jnp.where(low, a, turned(b)).astype(BF16)
            target[2 * pair + 1] = jnp.where(low, turned(a), b).astype(BF16)

    cot_copies = launch([to_chan(0, step, cot, cot_all.at[mine]) for step in range(1, chans)])
    cot_all[pl.ds(mine, 1)] = cot[...][None]
    pack(inputs, filters, first_send)
    first_copies = exchange(0, first_send, first_got)

    arrive(cot_copies)
    grad_gated = jnp.zeros((rows, cols), F32)
    for chan in range(chans):
        grad_gated = grad_gated + lax.dot_general(
            cot_all[chan], w_out[:, chan * cols : (chan + 1) * cols],
            (((1,), (1,)), ((), ())), preferred_element_type=F32,
        )
    pack(gate, grad_gated, second_send)
    second_copies = exchange(1, second_send, second_got)
    share = chans * cols // parts
    for part in range(parts):
        chan, start = divmod(part * share, cols)
        cot_send[part] = cot_all[chan, :, start : start + share]
    cot_col_copies = exchange(2, cot_send, cot_cols)

    own_taps = taps[:, pl.ds(pl.multiple_of(lax.div(me, 2) * LANES, LANES), LANES)]
    odd = jnp.full(own_taps.shape, lax.rem(me, 2), jnp.int32) == 1
    own_taps = jnp.where(odd, turned(own_taps), own_taps)
    tap_ids = lax.broadcasted_iota(jnp.int32, own_taps.shape, 0)
    mixing[...] = jnp.where(left_half(own_taps.shape), own_taps, (tap_ids == 0).astype(F32))

    arrive(first_copies)
    packed = first_got[...].reshape(tokens, LANES).astype(F32)
    mixed = packed * mixing[0:1, :]
    for tap in range(1, tap_count):
        mixed = mixed + mixing[tap : tap + 1, :] * moved(packed, tap)
    high, low = split_value(mixed)
    wide_short[:, :LANES] = high
    wide_short[:, LANES:] = low
    for table in tables:
        table.wait()
    wide_transform(fwd_high, fwd_low, wide_short, spec)

    def multiply(rows_at):
        other = pl.ds(pl.multiple_of(rows_at.start + tokens, TILE), TILE)
        real, imag = (spec[rows_at, :], spec[other, :])
        real_turned, imag_turned = (turned(real), turned(imag))
        half_long[rows_at, :] = packed_split(real * real_turned - imag * imag_turned)
        half_long[other, :] = packed_split(real * imag_turned + imag * real_turned)

    tiles(tokens, multiply)
    half_transform(inv_high, inv_low, half_long, signal)

    arrive(second_copies)
    for part in range(parts):
        span = slice(part * rows, (part + 1) * rows)
        branch = second_got[part].astype(F32)
        scaled = branch * signal[span, :]
        gated_all[pl.ds(me, 1), :, span] = scaled.T[:HALF].astype(BF16)[None]
        gate_send[part] = jnp.where(
            left_half((rows // 2, LANES)), turned(scaled[: rows // 2]), scaled[rows // 2 :]
        ).astype(BF16)
        half_short[span, :] = packed_split(branch * turned(branch))

    line = [
        to_seq(3, step, gated_all.at[me], gated_all.at[me]) for step in range(1, parts)
    ]
    launch(line)
    gate_copies = exchange(4, gate_send, gate_got)

    half_transform(fwd_high, fwd_low, half_short, grad_spec)

    def back(rows_at):
        other = pl.ds(pl.multiple_of(rows_at.start + tokens, TILE), TILE)
        real, imag = (turned(spec[rows_at, :]), turned(spec[other, :]))
        grad_real, grad_imag = (grad_spec[rows_at, :], grad_spec[other, :])
        high, low = split_value(real * grad_real + imag * grad_imag)
        wide_long[rows_at, :LANES] = high
        wide_long[rows_at, LANES:] = low
        high, low = split_value(real * grad_imag - imag * grad_real)
        wide_long[other, :LANES] = high
        wide_long[other, LANES:] = low

    tiles(tokens, back)
    wide_transform(inv_high, inv_low, wide_long, signal)
    grads = signal[...]
    mixed_back = grads * mixing[0:1, :]
    packed = first_got[...].reshape(tokens, LANES).astype(F32)
    taps_send[...] = jnp.zeros_like(taps_send)
    for tap in range(tap_count):
        if tap:
            mixed_back = mixed_back + mixing[tap : tap + 1, :] * moved(grads, -tap)
        taps_send[tap : tap + 1, :] = jnp.sum(
            moved(packed, tap) * grads, axis=0, keepdims=True
        )
    third_send[...] = mixed_back.astype(BF16).reshape(parts, rows, LANES)
    third_copies = exchange(5, third_send, third_got)
    taps_copies = launch(
        [to_seq(6, step, taps_send, taps_got.at[me]) for step in range(1, parts)]
    )
    taps_got[pl.ds(me, 1)] = taps_send[...][None]

    arrive(line)
    here = pl.ds(pl.multiple_of(me * rows, rows), rows)
    own_gated = gated_all[:, :, here].astype(F32).reshape(parts * HALF, rows).T.astype(BF16)
    for chan in range(chans):
        part_send[chan] = product(own_gated, w_out[:, chan * cols : (chan + 1) * cols]).astype(BF16)
    part_copies = launch(
        [
            to_chan(1, step, part_send.at[lax.rem(mine + step, chans)], part_got.at[mine])
            for step in range(1, chans)
        ]
    )
    part_got[pl.ds(mine, 1)] = part_send[pl.ds(mine, 1)]

    arrive(cot_col_copies)
    grad_wout[...] = product(
        gated_all[...].reshape(parts * HALF, tokens), cot_cols[...].reshape(tokens, share)
    )
    arrive(gate_copies)
    arrive(third_copies)
    arrive(taps_copies)
    for pair in range(parts // 2):
        span = slice(pair * LANES, (pair + 1) * LANES)
        a, b = (third_got[2 * pair].astype(F32), third_got[2 * pair + 1].astype(F32))
        low = left_half(a.shape)
        grad_inputs[:, span] = jnp.where(low, a, turned(b)).astype(BF16)
        grad_filters[:, span] = jnp.where(low, turned(a), b)
        a, b = (gate_got[2 * pair].astype(F32), gate_got[2 * pair + 1].astype(F32))
        low = left_half(a.shape)
        grad_gate[: rows // 2, span] = jnp.where(low, a, turned(b)).astype(BF16)
        grad_gate[rows // 2 :, span] = jnp.where(low, turned(a), b).astype(BF16)
        a, b = (taps_got[2 * pair], taps_got[2 * pair + 1])
        grad_taps[:, span] = jnp.where(left_half(a.shape), a, turned(b))[:tap_count]

    arrive(part_copies)
    total = part_got[0].astype(F32)
    for chan in range(1, chans):
        total = total + part_got[chan].astype(F32)
    output[...] = total.astype(BF16)
    for copies in (
        cot_copies, first_copies, second_copies, cot_col_copies, line, gate_copies,
        third_copies, taps_copies, part_copies,
    ):
        for copy in copies:
            copy.wait_send()


def dense_local(inputs, gate_branch, short_taps, filters, w_out, cotangent):
    parts = lax.axis_size("seq")
    chans = lax.axis_size("chan")
    rows, cols = inputs.shape
    tokens = rows * parts
    share = cols * chans // parts
    tap_rows = 8
    (fwd_high, fwd_low), (inv_high, inv_low) = dense_tables(tokens)
    vmem = pl.BlockSpec(memory_space=pltpu.VMEM)
    hbm = pl.BlockSpec(memory_space=pl.ANY)
    shape = jax.ShapeDtypeStruct
    return pl.pallas_call(
        block_kernel,
        out_shape=(
            shape((rows, cols), BF16), shape((rows, cols), BF16), shape((rows, cols), BF16),
            shape((rows, cols), F32), shape(short_taps.shape, F32), shape((cols, share), F32),
        ),
        in_specs=[vmem] * 6 + [hbm] * 4,
        out_specs=[vmem] * 6,
        scratch_shapes=[
            pltpu.VMEM((2 * tokens, tokens), BF16), pltpu.VMEM((2 * tokens, tokens), BF16),
            pltpu.VMEM((tokens, 2 * tokens), BF16), pltpu.VMEM((tokens, 2 * tokens), BF16),
            pltpu.VMEM((chans, rows, cols), BF16),
            pltpu.VMEM((parts, rows, share), BF16), pltpu.VMEM((parts, rows, share), BF16),
            pltpu.VMEM((parts, rows, LANES), BF16), pltpu.VMEM((parts, rows, LANES), BF16),
            pltpu.VMEM((parts, rows, LANES), BF16), pltpu.VMEM((parts, rows, LANES), BF16),
            pltpu.VMEM((parts, HALF, tokens), BF16),
            pltpu.VMEM((parts, rows, LANES), BF16), pltpu.VMEM((parts, rows, LANES), BF16),
            pltpu.VMEM((parts, rows // 2, LANES), BF16), pltpu.VMEM((parts, rows // 2, LANES), BF16),
            pltpu.VMEM((tap_rows, LANES), F32), pltpu.VMEM((parts, tap_rows, LANES), F32),
            pltpu.VMEM((chans, rows, cols), BF16), pltpu.VMEM((chans, rows, cols), BF16),
            pltpu.VMEM((tokens, 2 * LANES), BF16), pltpu.VMEM((tokens, LANES), BF16),
            pltpu.VMEM((2 * tokens, LANES), BF16), pltpu.VMEM((2 * tokens, 2 * LANES), BF16),
            pltpu.VMEM((2 * tokens, LANES), F32), pltpu.VMEM((2 * tokens, LANES), F32),
            pltpu.VMEM((tokens, LANES), F32), pltpu.VMEM((short_taps.shape[0], LANES), F32),
            pltpu.SemaphoreType.DMA((4,)),
            pltpu.SemaphoreType.DMA((7, parts)), pltpu.SemaphoreType.DMA((7, parts)),
            pltpu.SemaphoreType.DMA((2, chans)), pltpu.SemaphoreType.DMA((2, chans)),
        ],
        compiler_params=pltpu.CompilerParams(
            collective_id=0, has_side_effects=True, vmem_limit_bytes=56 * 1024 * 1024
        ),
    )(inputs, gate_branch, short_taps, filters, w_out, cotangent, fwd_high, fwd_low, inv_high, inv_low)


def local(inputs, *others):
    parts = lax.axis_size("seq")
    rows, cols = inputs.shape
    fits = rows * parts <= DENSE_TOKENS and rows % LANES == 0 and cols == HALF * parts
    return (dense_local if fits else panel_local)(inputs, *others)


def solution(mesh):
    in_specs = (
        P("seq", "chan"),
        P("seq", "chan"),
        P(None, "chan"),
        P("seq", "chan"),
        P("chan", None),
        P("seq", "chan"),
    )
    out_specs = (
        P("seq", "chan"),
        P("seq", "chan"),
        P("seq", "chan"),
        P("seq", "chan"),
        P(None, "chan"),
        P("chan", "seq"),
    )
    return jax.shard_map(local, mesh=mesh, in_specs=in_specs, out_specs=out_specs, check_vma=False)
```

```python
import math

import functools

import jax
import jax.numpy as jnp
import numpy as np
from jax import lax
from jax.experimental import pallas as pl
from jax.experimental.pallas import tpu as pltpu
from jax.sharding import PartitionSpec as P

HIGHEST = lax.Precision.HIGHEST


def from_behind(value, axis, steps):
    count = lax.axis_size(axis)
    first, last = (max(0, -steps), min(count, count - steps))
    return lax.ppermute(value, axis, [(source, source + steps) for source in range(first, last)])


def angle_table(row_len, col_len, modulus, row_start, col_start, direction):
    row_ids = lax.iota(jnp.int32, row_len)[:, None] + row_start
    col_ids = lax.iota(jnp.int32, col_len)[None, :] + col_start
    phase = row_ids * col_ids % modulus
    angles = phase.astype(jnp.float32) * (direction * 2.0 * math.pi / modulus)
    return (jnp.cos(angles), jnp.sin(angles))


def column_dft(real_part, imag_part, length, form, direction):
    cos_table, sin_table = angle_table(length, length, length, 0, 0, direction)
    new_real = jnp.einsum(form, real_part, cos_table, precision=HIGHEST) - jnp.einsum(
        form, imag_part, sin_table, precision=HIGHEST
    )
    new_imag = jnp.einsum(form, real_part, sin_table, precision=HIGHEST) + jnp.einsum(
        form, imag_part, cos_table, precision=HIGHEST
    )
    return (new_real, new_imag)


def panel_forward(signal):
    stack_size = signal.shape[0]
    block_len = signal.shape[1]
    part_count = lax.axis_size("seq")
    my_index = lax.axis_index("seq")
    narrow = block_len // part_count
    row_order = 2 * part_count
    full_len = row_order * block_len
    by_column = lax.all_to_all(signal[:, None], "seq", split_axis=2, concat_axis=1, tiled=True)
    row_cos, row_sin = angle_table(row_order, part_count, row_order, 0, 0, -1.0)
    real_part = jnp.einsum("ja,kabf->kjbf", row_cos, by_column, precision=HIGHEST)
    imag_part = jnp.einsum("ja,kabf->kjbf", row_sin, by_column, precision=HIGHEST)
    twist_cos, twist_sin = angle_table(row_order, narrow, full_len, 0, my_index * narrow, -1.0)
    twist_cos = twist_cos[None, :, :, None]
    twist_sin = twist_sin[None, :, :, None]
    real_twist = real_part * twist_cos - imag_part * twist_sin
    imag_twist = real_part * twist_sin + imag_part * twist_cos
    by_rows = lax.all_to_all(
        jnp.concatenate([real_twist, imag_twist], 0), "seq", split_axis=1, concat_axis=2, tiled=True
    )
    return column_dft(by_rows[:stack_size], by_rows[stack_size:], block_len, "kjbf,bm->kjmf", -1.0)


def panel_inverse(real_part, imag_part):
    stack_size = real_part.shape[0]
    block_len = real_part.shape[2]
    part_count = lax.axis_size("seq")
    my_index = lax.axis_index("seq")
    row_order = 2 * part_count
    full_len = row_order * block_len
    real_back, imag_back = column_dft(real_part, imag_part, block_len, "kjmf,mb->kjbf", 1.0)
    twist_cos, twist_sin = angle_table(2, block_len, full_len, my_index * 2, 0, 1.0)
    twist_cos = twist_cos[None, :, :, None]
    twist_sin = twist_sin[None, :, :, None]
    real_twist = (real_back * twist_cos - imag_back * twist_sin) / block_len
    imag_twist = (real_back * twist_sin + imag_back * twist_cos) / block_len
    by_column = lax.all_to_all(
        jnp.concatenate([real_twist, imag_twist], 0), "seq", split_axis=2, concat_axis=1, tiled=True
    )
    row_cos, row_sin = angle_table(part_count, row_order, row_order, 0, 0, 1.0)
    signal = (
        jnp.einsum("aj,kjbf->kabf", row_cos, by_column[:stack_size], precision=HIGHEST)
        - jnp.einsum("aj,kjbf->kabf", row_sin, by_column[stack_size:], precision=HIGHEST)
    ) / row_order
    returned = lax.all_to_all(signal, "seq", split_axis=1, concat_axis=2, tiled=True)
    return returned[:, 0]


def panel_local(inputs, gate_branch, short_taps, filters, w_out, cotangent):
    forward_fn, inverse_fn = (panel_forward, panel_inverse)
    tap_count = short_taps.shape[0]
    row_count = inputs.shape[0]
    left_tail = from_behind(inputs[row_count - (tap_count - 1) :], "seq", 1)
    extended = jnp.concatenate([left_tail, inputs], 0).astype(jnp.float32)
    mixed = jnp.zeros((row_count, inputs.shape[1]), jnp.float32)
    for tap_index in range(tap_count):
        start_row = tap_count - 1 - tap_index
        mixed = mixed + short_taps[tap_index] * extended[start_row : start_row + row_count]
    spec_real, spec_imag = forward_fn(jnp.stack([mixed, filters], 0))
    mixed_real, filter_real = (spec_real[0], spec_real[1])
    mixed_imag, filter_imag = (spec_imag[0], spec_imag[1])
    prod_real = mixed_real * filter_real - mixed_imag * filter_imag
    prod_imag = mixed_real * filter_imag + mixed_imag * filter_real
    convolved = inverse_fn(prod_real[None], prod_imag[None])[0]
    gate_wide = gate_branch.astype(jnp.float32)
    gated = (gate_wide * convolved).astype(jnp.bfloat16)
    out_terms = jnp.dot(gated, w_out, preferred_element_type=jnp.float32)
    output = lax.psum_scatter(out_terms, "chan", scatter_dimension=1, tiled=True).astype(
        jnp.bfloat16
    )
    full_cot = lax.all_gather(cotangent, "chan", axis=1, tiled=True)
    grad_gated = lax.dot_general(
        full_cot, w_out, (((1,), (1,)), ((), ())), preferred_element_type=jnp.float32
    )
    grad_gate = (grad_gated * convolved).astype(jnp.bfloat16)
    grad_conv = grad_gated * gate_wide
    grad_real, grad_imag = forward_fn(grad_conv[None])
    grad_real = grad_real[0]
    grad_imag = grad_imag[0]
    back_real = jnp.stack(
        [
            filter_real * grad_real + filter_imag * grad_imag,
            mixed_real * grad_real + mixed_imag * grad_imag,
        ],
        0,
    )
    back_imag = jnp.stack(
        [
            filter_real * grad_imag - filter_imag * grad_real,
            mixed_real * grad_imag - mixed_imag * grad_real,
        ],
        0,
    )
    gradients = inverse_fn(back_real, back_imag)
    grad_mixed = gradients[0]
    grad_filters = gradients[1]
    right_head = from_behind(grad_mixed[: tap_count - 1], "seq", -1)
    grad_ext = jnp.concatenate([grad_mixed, right_head], 0)
    grad_wide = jnp.zeros_like(grad_mixed)
    tap_rows = []
    for tap_index in range(tap_count):
        start_row = tap_count - 1 - tap_index
        grad_wide = grad_wide + short_taps[tap_index] * grad_ext[tap_index : tap_index + row_count]
        tap_rows.append(jnp.sum(extended[start_row : start_row + row_count] * grad_mixed, axis=0))
    grad_inputs = grad_wide.astype(jnp.bfloat16)
    grad_taps = lax.psum(jnp.stack(tap_rows, 0), "seq")
    weight_terms = lax.dot_general(
        gated, full_cot, (((0,), (0,)), ((), ())), preferred_element_type=jnp.float32
    )
    grad_wout = lax.psum_scatter(weight_terms, "seq", scatter_dimension=1, tiled=True)
    return (output, grad_inputs, grad_gate, grad_filters, grad_taps, grad_wout)


DENSE_TOKENS = 2048


def split_table(table):
    high = table.astype(jnp.bfloat16)
    low = (table - high.astype(np.float64)).astype(jnp.bfloat16)
    return (high, low)


def dense_tables(tokens):
    freq = np.arange(tokens, dtype=np.int64)[:, None]
    time = np.arange(tokens, dtype=np.int64)[None, :]
    angles = ((2 * freq + 1) * time % (4 * tokens)) * (2.0 * np.pi / (4 * tokens))
    forward = np.concatenate([np.cos(angles), -np.sin(angles)], 0)
    inverse = forward.T / tokens
    return (split_table(forward), split_table(inverse))


LANES = 128
HALF = 64
TILE = 256
DOT_TILE = 512
BF16 = jnp.bfloat16
F32 = jnp.float32


def left_half(shape):
    return lax.broadcasted_iota(jnp.int32, shape, 1) < HALF


def turned(value):
    return pltpu.roll(value, HALF, 1)


def split_value(value):
    high = value.astype(BF16)
    return (high, (value - high.astype(F32)).astype(BF16))


def packed_split(value):
    high = value.astype(BF16).astype(F32)
    return jnp.where(left_half(value.shape), high, value - high).astype(BF16)


def tiles(count, body, size=TILE):
    def step(index, carry):
        body(pl.ds(pl.multiple_of(index * size, size), size))
        return carry

    lax.fori_loop(0, count // size, step, 0)


def product(left, right):
    return jnp.dot(left, right, preferred_element_type=F32)


def wide_transform(high, low, value, result):
    def body(rows):
        first = product(high[rows, :], value[...])
        second = product(low[rows, :], value[:, :LANES])
        result[rows, :] = first[:, :LANES] + first[:, LANES:] + second

    tiles(result.shape[0], body, DOT_TILE)


def half_transform(high, low, value, result):
    def body(rows):
        total = product(high[rows, :], value[...]) + product(low[rows, :], value[...])
        result[rows, :] = total + turned(total)

    tiles(result.shape[0], body, DOT_TILE)


def moved(value, steps):
    if steps == 0:
        return value
    count = value.shape[0]
    row = lax.broadcasted_iota(jnp.int32, value.shape, 0)
    keep = (row >= steps) if steps > 0 else (row < count + steps)
    return jnp.where(keep, pltpu.roll(value, steps % count, 0), 0.0)


def block_kernel(
    inputs, gate, taps, filters, w_out_hbm, cot, fwd_high_hbm, fwd_low_hbm, inv_high_hbm, inv_low_hbm,
    output, grad_inputs, grad_gate, grad_filters, grad_taps, grad_wout,
    w_out, fwd_high, fwd_low, inv_high, inv_low, cot_all, cot_send, cot_cols, first_send, first_got,
    second_send, second_got, gated_all, own_got, third_send, third_got, gate_send, gate_got,
    taps_send, taps_got, part_send, part_got, wide_short, half_short, half_long, wide_long,
    spec, grad_spec, signal, mixing, table_sems, send_sems, recv_sems, chan_send_sems, chan_recv_sems,
):
    parts, rows = first_got.shape[0], first_got.shape[1]
    chans, cols = cot_all.shape[0], inputs.shape[1]
    tokens = parts * rows
    tap_count = taps.shape[0]
    me = lax.axis_index("seq")
    mine = lax.axis_index("chan")

    tables = [
        pltpu.make_async_copy(source, target, table_sems.at[index])
        for index, (source, target) in enumerate(
            [
                (w_out_hbm, w_out), (fwd_high_hbm, fwd_high), (fwd_low_hbm, fwd_low),
                (inv_high_hbm, inv_high), (inv_low_hbm, inv_low),
            ]
        )
    ]
    for table in tables:
        table.start()

    barrier = pltpu.get_barrier_semaphore()
    for step in range(1, parts):
        pl.semaphore_signal(
            barrier, inc=1, device_id=(lax.rem(me + step, parts), mine),
            device_id_type=pl.DeviceIdType.MESH,
        )
    for step in range(1, chans):
        pl.semaphore_signal(
            barrier, inc=1, device_id=(me, lax.rem(mine + step, chans)),
            device_id_type=pl.DeviceIdType.MESH,
        )
    pl.semaphore_wait(barrier, parts + chans - 2)

    def to_seq(kind, step, source, target):
        return pltpu.make_async_remote_copy(
            src_ref=source, dst_ref=target,
            send_sem=send_sems.at[kind, step], recv_sem=recv_sems.at[kind, step],
            device_id=(lax.rem(me + step, parts), mine), device_id_type=pl.DeviceIdType.MESH,
        )

    def to_chan(kind, step, source, target):
        return pltpu.make_async_remote_copy(
            src_ref=source, dst_ref=target,
            send_sem=chan_send_sems.at[kind, step], recv_sem=chan_recv_sems.at[kind, step],
            device_id=(me, lax.rem(mine + step, chans)), device_id_type=pl.DeviceIdType.MESH,
        )

    def launch(copies):
        for copy in copies:
            copy.start()
        return copies

    def arrive(copies):
        for copy in copies:
            copy.wait_recv()

    def exchange(kind, sent, got):
        copies = launch(
            [
                to_seq(kind, step, sent.at[lax.rem(me + step, parts)], got.at[me])
                for step in range(1, parts)
            ]
        )
        got[pl.ds(me, 1)] = sent[pl.ds(me, 1)]
        return copies

    def pack(left, right, target):
        for pair in range(parts // 2):
            span = slice(pair * LANES, (pair + 1) * LANES)
            a, b = (left[:, span].astype(F32), right[:, span].astype(F32))
            low = left_half(a.shape)
            target[2 * pair] = jnp.where(low, a, turned(b)).astype(BF16)
            target[2 * pair + 1] = jnp.where(low, turned(a), b).astype(BF16)

    cot_copies = launch([to_chan(0, step, cot, cot_all.at[mine]) for step in range(1, chans)])
    cot_all[pl.ds(mine, 1)] = cot[...][None]
    pack(inputs, filters, first_send)
    first_copies = exchange(0, first_send, first_got)

    arrive(cot_copies)
    tables[0].wait()
    grad_gated = jnp.zeros((rows, cols), F32)
    for chan in range(chans):
        grad_gated = grad_gated + lax.dot_general(
            cot_all[chan], w_out[:, chan * cols : (chan + 1) * cols],
            (((1,), (1,)), ((), ())), preferred_element_type=F32,
        )
    pack(gate, grad_gated, second_send)
    second_copies = exchange(1, second_send, second_got)
    share = chans * cols // parts
    quarter_rows = rows // chans
    quarter = pl.ds(pl.multiple_of(mine * quarter_rows, quarter_rows), quarter_rows)
    for part in range(parts):
        chan, start = divmod(part * share, cols)
        cot_send[part] = cot_all[chan, quarter, start : start + share]
    cot_col_copies = launch(
        [
            to_seq(
                2, step, cot_send.at[lax.rem(me + step, parts)], cot_cols.at[me, quarter]
            )
            for step in range(1, parts)
        ]
    )
    cot_cols[pl.ds(me, 1), quarter] = cot_send[pl.ds(me, 1)]

    own_taps = taps[:, pl.ds(pl.multiple_of(lax.div(me, 2) * LANES, LANES), LANES)]
    odd = jnp.full(own_taps.shape, lax.rem(me, 2), jnp.int32) == 1
    own_taps = jnp.where(odd, turned(own_taps), own_taps)
    tap_ids = lax.broadcasted_iota(jnp.int32, own_taps.shape, 0)
    mixing[...] = jnp.where(left_half(own_taps.shape), own_taps, (tap_ids == 0).astype(F32))

    arrive(first_copies)
    packed = first_got[...].reshape(tokens, LANES).astype(F32)
    mixed = packed * mixing[0:1, :]
    for tap in range(1, tap_count):
        mixed = mixed + mixing[tap : tap + 1, :] * moved(packed, tap)
    high, low = split_value(mixed)
    wide_short[:, :LANES] = high
    wide_short[:, LANES:] = low
    for table in tables[1:]:
        table.wait()
    wide_transform(fwd_high, fwd_low, wide_short, spec)

    def multiply(rows_at):
        other = pl.ds(pl.multiple_of(rows_at.start + tokens, TILE), TILE)
        real, imag = (spec[rows_at, :], spec[other, :])
        real_turned, imag_turned = (turned(real), turned(imag))
        half_long[rows_at, :] = packed_split(real * real_turned - imag * imag_turned)
        half_long[other, :] = packed_split(real * imag_turned + imag * real_turned)

    tiles(tokens, multiply)
    half_transform(inv_high, inv_low, half_long, signal)

    arrive(cot_col_copies)
    cot_row_copies = launch(
        [
            to_chan(2, step, cot_cols.at[:, quarter], cot_cols.at[:, quarter])
            for step in range(1, chans)
        ]
    )
    arrive(second_copies)
    for part in range(parts):
        span = slice(part * rows, (part + 1) * rows)
        branch = second_got[part].astype(F32)
        scaled = branch * signal[span, :]
        gated_all[pl.ds(me, 1), :, span] = scaled.T[:HALF].astype(BF16)[None]
        gate_send[part] = jnp.where(
            left_half((rows // 2, LANES)), turned(scaled[: rows // 2]), scaled[rows // 2 :]
        ).astype(BF16)
        half_short[span, :] = packed_split(branch * turned(branch))

    own_copies = launch(
        [
            to_seq(
                7, step,
                gated_all.at[
                    me, :, pl.ds(pl.multiple_of(lax.rem(me + step, parts) * rows, rows), rows)
                ],
                own_got.at[me],
            )
            for step in range(1, parts)
        ]
    )
    here = pl.ds(pl.multiple_of(me * rows, rows), rows)
    own_got[pl.ds(me, 1)] = gated_all[pl.ds(me, 1), :, here]
    line = launch(
        [to_seq(3, step, gated_all.at[me], gated_all.at[me]) for step in range(2, parts, 2)]
    )
    partner = me + 1 - 2 * lax.rem(me, 2)

    def hand_on(step):
        source = lax.rem(me + parts - step, parts)
        return pltpu.make_async_remote_copy(
            src_ref=gated_all.at[source], dst_ref=gated_all.at[source],
            send_sem=send_sems.at[8, step], recv_sem=recv_sems.at[8, step],
            device_id=(partner, mine), device_id_type=pl.DeviceIdType.MESH,
        )

    handed = launch([hand_on(0)])
    gate_copies = exchange(4, gate_send, gate_got)

    half_transform(fwd_high, fwd_low, half_short, grad_spec)

    arrive(own_copies)
    own_gated = own_got[...].astype(F32).reshape(parts * HALF, rows).T.astype(BF16)
    for chan in range(chans):
        part_send[chan] = product(own_gated, w_out[:, chan * cols : (chan + 1) * cols]).astype(BF16)
    part_copies = launch(
        [
            to_chan(1, step, part_send.at[lax.rem(mine + step, chans)], part_got.at[mine])
            for step in range(1, chans)
        ]
    )
    part_got[pl.ds(mine, 1)] = part_send[pl.ds(mine, 1)]

    for step, copy in zip(range(2, parts, 2), line):
        copy.wait_recv()
        handed += launch([hand_on(step)])

    def back(rows_at):
        other = pl.ds(pl.multiple_of(rows_at.start + tokens, TILE), TILE)
        real, imag = (turned(spec[rows_at, :]), turned(spec[other, :]))
        grad_real, grad_imag = (grad_spec[rows_at, :], grad_spec[other, :])
        high, low = split_value(real * grad_real + imag * grad_imag)
        wide_long[rows_at, :LANES] = high
        wide_long[rows_at, LANES:] = low
        high, low = split_value(real * grad_imag - imag * grad_real)
        wide_long[other, :LANES] = high
        wide_long[other, LANES:] = low

    tiles(tokens, back)
    wide_transform(inv_high, inv_low, wide_long, signal)
    grads = signal[...]
    mixed_back = grads * mixing[0:1, :]
    packed = first_got[...].reshape(tokens, LANES).astype(F32)
    taps_send[...] = jnp.zeros_like(taps_send)
    for tap in range(tap_count):
        if tap:
            mixed_back = mixed_back + mixing[tap : tap + 1, :] * moved(grads, -tap)
        taps_send[tap : tap + 1, :] = jnp.sum(
            moved(packed, tap) * grads, axis=0, keepdims=True
        )
    third_send[...] = mixed_back.astype(BF16).reshape(parts, rows, LANES)
    third_copies = exchange(5, third_send, third_got)
    taps_copies = launch(
        [to_seq(6, step, taps_send, taps_got.at[me]) for step in range(1, parts)]
    )
    taps_got[pl.ds(me, 1)] = taps_send[...][None]

    arrive(cot_row_copies)
    arrive(handed)
    grad_wout[...] = product(
        gated_all[...].reshape(parts * HALF, tokens), cot_cols[...].reshape(tokens, share)
    )
    arrive(gate_copies)
    arrive(third_copies)
    arrive(taps_copies)
    for pair in range(parts // 2):
        span = slice(pair * LANES, (pair + 1) * LANES)
        a, b = (third_got[2 * pair].astype(F32), third_got[2 * pair + 1].astype(F32))
        low = left_half(a.shape)
        grad_inputs[:, span] = jnp.where(low, a, turned(b)).astype(BF16)
        grad_filters[:, span] = jnp.where(low, turned(a), b)
        a, b = (gate_got[2 * pair].astype(F32), gate_got[2 * pair + 1].astype(F32))
        low = left_half(a.shape)
        grad_gate[: rows // 2, span] = jnp.where(low, a, turned(b)).astype(BF16)
        grad_gate[rows // 2 :, span] = jnp.where(low, turned(a), b).astype(BF16)
        a, b = (taps_got[2 * pair], taps_got[2 * pair + 1])
        grad_taps[:, span] = jnp.where(left_half(a.shape), a, turned(b))[:tap_count]

    arrive(part_copies)
    total = part_got[0].astype(F32)
    for chan in range(1, chans):
        total = total + part_got[chan].astype(F32)
    output[...] = total.astype(BF16)
    for copies in (
        cot_copies, first_copies, second_copies, cot_col_copies, cot_row_copies, own_copies, line,
        handed, gate_copies, third_copies, taps_copies, part_copies,
    ):
        for copy in copies:
            copy.wait_send()


def store_kernel(*refs):
    sems = refs[-1]
    count = sems.shape[0]
    copies = [
        pltpu.make_async_copy(refs[index], refs[count + index], sems.at[index])
        for index in range(count)
    ]
    for copy in copies:
        copy.start()
    for copy in copies:
        copy.wait()


def dense_local(inputs, gate_branch, short_taps, filters, w_out, cotangent):
    parts = lax.axis_size("seq")
    chans = lax.axis_size("chan")
    rows, cols = inputs.shape
    tokens = rows * parts
    share = cols * chans // parts
    tap_rows = 8
    (fwd_high, fwd_low), (inv_high, inv_low) = dense_tables(tokens)
    vmem = pl.BlockSpec(memory_space=pltpu.VMEM)
    hbm = pl.BlockSpec(memory_space=pl.ANY)
    shape = jax.ShapeDtypeStruct
    results = pl.pallas_call(
        block_kernel,
        out_shape=(
            shape((rows, cols), BF16), shape((rows, cols), BF16), shape((rows, cols), BF16),
            shape((rows, cols), F32), shape(short_taps.shape, F32), shape((cols, share), F32),
        ),
        in_specs=[vmem] * 4 + [hbm, vmem] + [hbm] * 4,
        out_specs=[vmem] * 6,
        scratch_shapes=[
            pltpu.VMEM(w_out.shape, BF16),
            pltpu.VMEM((2 * tokens, tokens), BF16), pltpu.VMEM((2 * tokens, tokens), BF16),
            pltpu.VMEM((tokens, 2 * tokens), BF16), pltpu.VMEM((tokens, 2 * tokens), BF16),
            pltpu.VMEM((chans, rows, cols), BF16),
            pltpu.VMEM((parts, rows // chans, share), BF16), pltpu.VMEM((parts, rows, share), BF16),
            pltpu.VMEM((parts, rows, LANES), BF16), pltpu.VMEM((parts, rows, LANES), BF16),
            pltpu.VMEM((parts, rows, LANES), BF16), pltpu.VMEM((parts, rows, LANES), BF16),
            pltpu.VMEM((parts, HALF, tokens), BF16), pltpu.VMEM((parts, HALF, rows), BF16),
            pltpu.VMEM((parts, rows, LANES), BF16), pltpu.VMEM((parts, rows, LANES), BF16),
            pltpu.VMEM((parts, rows // 2, LANES), BF16), pltpu.VMEM((parts, rows // 2, LANES), BF16),
            pltpu.VMEM((tap_rows, LANES), F32), pltpu.VMEM((parts, tap_rows, LANES), F32),
            pltpu.VMEM((chans, rows, cols), BF16), pltpu.VMEM((chans, rows, cols), BF16),
            pltpu.VMEM((tokens, 2 * LANES), BF16), pltpu.VMEM((tokens, LANES), BF16),
            pltpu.VMEM((2 * tokens, LANES), BF16), pltpu.VMEM((2 * tokens, 2 * LANES), BF16),
            pltpu.VMEM((2 * tokens, LANES), F32), pltpu.VMEM((2 * tokens, LANES), F32),
            pltpu.VMEM((tokens, LANES), F32), pltpu.VMEM((short_taps.shape[0], LANES), F32),
            pltpu.SemaphoreType.DMA((5,)),
            pltpu.SemaphoreType.DMA((9, parts)), pltpu.SemaphoreType.DMA((9, parts)),
            pltpu.SemaphoreType.DMA((3, chans)), pltpu.SemaphoreType.DMA((3, chans)),
        ],
        compiler_params=pltpu.CompilerParams(
            collective_id=0, has_side_effects=True, vmem_limit_bytes=56 * 1024 * 1024
        ),
    )(inputs, gate_branch, short_taps, filters, w_out, cotangent, fwd_high, fwd_low, inv_high, inv_low)
    count = len(results)
    return pl.pallas_call(
        store_kernel,
        out_shape=[shape(value.shape, value.dtype) for value in results],
        in_specs=[hbm] * count,
        out_specs=[hbm] * count,
        scratch_shapes=[pltpu.SemaphoreType.DMA((count,))],
    )(*results)


def local(inputs, *others):
    parts = lax.axis_size("seq")
    rows, cols = inputs.shape
    fits = rows * parts <= DENSE_TOKENS and rows % LANES == 0 and parts % 2 == 0
    fits = fits and cols == HALF * parts and rows % (16 * lax.axis_size("chan")) == 0
    return (dense_local if fits else panel_local)(inputs, *others)


def solution(mesh):
    in_specs = (
        P("seq", "chan"),
        P("seq", "chan"),
        P(None, "chan"),
        P("seq", "chan"),
        P("chan", None),
        P("seq", "chan"),
    )
    out_specs = (
        P("seq", "chan"),
        P("seq", "chan"),
        P("seq", "chan"),
        P("seq", "chan"),
        P(None, "chan"),
        P("chan", "seq"),
    )
    return jax.shard_map(local, mesh=mesh, in_specs=in_specs, out_specs=out_specs, check_vma=False)
```

```python
import math

import functools

import jax
import jax.numpy as jnp
import numpy as np
from jax import lax
from jax.experimental import pallas as pl
from jax.experimental.pallas import tpu as pltpu
from jax.sharding import PartitionSpec as P

HIGHEST = lax.Precision.HIGHEST


def from_behind(value, axis, steps):
    count = lax.axis_size(axis)
    first, last = (max(0, -steps), min(count, count - steps))
    return lax.ppermute(value, axis, [(source, source + steps) for source in range(first, last)])


def angle_table(row_len, col_len, modulus, row_start, col_start, direction):
    row_ids = lax.iota(jnp.int32, row_len)[:, None] + row_start
    col_ids = lax.iota(jnp.int32, col_len)[None, :] + col_start
    phase = row_ids * col_ids % modulus
    angles = phase.astype(jnp.float32) * (direction * 2.0 * math.pi / modulus)
    return (jnp.cos(angles), jnp.sin(angles))


def column_dft(real_part, imag_part, length, form, direction):
    cos_table, sin_table = angle_table(length, length, length, 0, 0, direction)
    new_real = jnp.einsum(form, real_part, cos_table, precision=HIGHEST) - jnp.einsum(
        form, imag_part, sin_table, precision=HIGHEST
    )
    new_imag = jnp.einsum(form, real_part, sin_table, precision=HIGHEST) + jnp.einsum(
        form, imag_part, cos_table, precision=HIGHEST
    )
    return (new_real, new_imag)


def panel_forward(signal):
    stack_size = signal.shape[0]
    block_len = signal.shape[1]
    part_count = lax.axis_size("seq")
    my_index = lax.axis_index("seq")
    narrow = block_len // part_count
    row_order = 2 * part_count
    full_len = row_order * block_len
    by_column = lax.all_to_all(signal[:, None], "seq", split_axis=2, concat_axis=1, tiled=True)
    row_cos, row_sin = angle_table(row_order, part_count, row_order, 0, 0, -1.0)
    real_part = jnp.einsum("ja,kabf->kjbf", row_cos, by_column, precision=HIGHEST)
    imag_part = jnp.einsum("ja,kabf->kjbf", row_sin, by_column, precision=HIGHEST)
    twist_cos, twist_sin = angle_table(row_order, narrow, full_len, 0, my_index * narrow, -1.0)
    twist_cos = twist_cos[None, :, :, None]
    twist_sin = twist_sin[None, :, :, None]
    real_twist = real_part * twist_cos - imag_part * twist_sin
    imag_twist = real_part * twist_sin + imag_part * twist_cos
    by_rows = lax.all_to_all(
        jnp.concatenate([real_twist, imag_twist], 0), "seq", split_axis=1, concat_axis=2, tiled=True
    )
    return column_dft(by_rows[:stack_size], by_rows[stack_size:], block_len, "kjbf,bm->kjmf", -1.0)


def panel_inverse(real_part, imag_part):
    stack_size = real_part.shape[0]
    block_len = real_part.shape[2]
    part_count = lax.axis_size("seq")
    my_index = lax.axis_index("seq")
    row_order = 2 * part_count
    full_len = row_order * block_len
    real_back, imag_back = column_dft(real_part, imag_part, block_len, "kjmf,mb->kjbf", 1.0)
    twist_cos, twist_sin = angle_table(2, block_len, full_len, my_index * 2, 0, 1.0)
    twist_cos = twist_cos[None, :, :, None]
    twist_sin = twist_sin[None, :, :, None]
    real_twist = (real_back * twist_cos - imag_back * twist_sin) / block_len
    imag_twist = (real_back * twist_sin + imag_back * twist_cos) / block_len
    by_column = lax.all_to_all(
        jnp.concatenate([real_twist, imag_twist], 0), "seq", split_axis=2, concat_axis=1, tiled=True
    )
    row_cos, row_sin = angle_table(part_count, row_order, row_order, 0, 0, 1.0)
    signal = (
        jnp.einsum("aj,kjbf->kabf", row_cos, by_column[:stack_size], precision=HIGHEST)
        - jnp.einsum("aj,kjbf->kabf", row_sin, by_column[stack_size:], precision=HIGHEST)
    ) / row_order
    returned = lax.all_to_all(signal, "seq", split_axis=1, concat_axis=2, tiled=True)
    return returned[:, 0]


def panel_local(inputs, gate_branch, short_taps, filters, w_out, cotangent):
    forward_fn, inverse_fn = (panel_forward, panel_inverse)
    tap_count = short_taps.shape[0]
    row_count = inputs.shape[0]
    left_tail = from_behind(inputs[row_count - (tap_count - 1) :], "seq", 1)
    extended = jnp.concatenate([left_tail, inputs], 0).astype(jnp.float32)
    mixed = jnp.zeros((row_count, inputs.shape[1]), jnp.float32)
    for tap_index in range(tap_count):
        start_row = tap_count - 1 - tap_index
        mixed = mixed + short_taps[tap_index] * extended[start_row : start_row + row_count]
    spec_real, spec_imag = forward_fn(jnp.stack([mixed, filters], 0))
    mixed_real, filter_real = (spec_real[0], spec_real[1])
    mixed_imag, filter_imag = (spec_imag[0], spec_imag[1])
    prod_real = mixed_real * filter_real - mixed_imag * filter_imag
    prod_imag = mixed_real * filter_imag + mixed_imag * filter_real
    convolved = inverse_fn(prod_real[None], prod_imag[None])[0]
    gate_wide = gate_branch.astype(jnp.float32)
    gated = (gate_wide * convolved).astype(jnp.bfloat16)
    out_terms = jnp.dot(gated, w_out, preferred_element_type=jnp.float32)
    output = lax.psum_scatter(out_terms, "chan", scatter_dimension=1, tiled=True).astype(
        jnp.bfloat16
    )
    full_cot = lax.all_gather(cotangent, "chan", axis=1, tiled=True)
    grad_gated = lax.dot_general(
        full_cot, w_out, (((1,), (1,)), ((), ())), preferred_element_type=jnp.float32
    )
    grad_gate = (grad_gated * convolved).astype(jnp.bfloat16)
    grad_conv = grad_gated * gate_wide
    grad_real, grad_imag = forward_fn(grad_conv[None])
    grad_real = grad_real[0]
    grad_imag = grad_imag[0]
    back_real = jnp.stack(
        [
            filter_real * grad_real + filter_imag * grad_imag,
            mixed_real * grad_real + mixed_imag * grad_imag,
        ],
        0,
    )
    back_imag = jnp.stack(
        [
            filter_real * grad_imag - filter_imag * grad_real,
            mixed_real * grad_imag - mixed_imag * grad_real,
        ],
        0,
    )
    gradients = inverse_fn(back_real, back_imag)
    grad_mixed = gradients[0]
    grad_filters = gradients[1]
    right_head = from_behind(grad_mixed[: tap_count - 1], "seq", -1)
    grad_ext = jnp.concatenate([grad_mixed, right_head], 0)
    grad_wide = jnp.zeros_like(grad_mixed)
    tap_rows = []
    for tap_index in range(tap_count):
        start_row = tap_count - 1 - tap_index
        grad_wide = grad_wide + short_taps[tap_index] * grad_ext[tap_index : tap_index + row_count]
        tap_rows.append(jnp.sum(extended[start_row : start_row + row_count] * grad_mixed, axis=0))
    grad_inputs = grad_wide.astype(jnp.bfloat16)
    grad_taps = lax.psum(jnp.stack(tap_rows, 0), "seq")
    weight_terms = lax.dot_general(
        gated, full_cot, (((0,), (0,)), ((), ())), preferred_element_type=jnp.float32
    )
    grad_wout = lax.psum_scatter(weight_terms, "seq", scatter_dimension=1, tiled=True)
    return (output, grad_inputs, grad_gate, grad_filters, grad_taps, grad_wout)


DENSE_TOKENS = 2048


def split_table(table):
    high = table.astype(jnp.bfloat16)
    low = (table - high.astype(np.float64)).astype(jnp.bfloat16)
    return (high, low)


def dense_tables(tokens):
    freq = np.arange(tokens, dtype=np.int64)[:, None]
    time = np.arange(tokens, dtype=np.int64)[None, :]
    angles = ((2 * freq + 1) * time % (4 * tokens)) * (2.0 * np.pi / (4 * tokens))
    forward = np.concatenate([np.cos(angles), -np.sin(angles)], 0)
    inverse = forward.T / tokens
    return (split_table(forward), split_table(inverse))


LANES = 128
HALF = 64
TILE = 256
DOT_TILE = 512
BF16 = jnp.bfloat16
F32 = jnp.float32


def left_half(shape):
    return lax.broadcasted_iota(jnp.int32, shape, 1) < HALF


def turned(value):
    return pltpu.roll(value, HALF, 1)


def split_value(value):
    high = value.astype(BF16)
    return (high, (value - high.astype(F32)).astype(BF16))


def packed_split(value):
    high = value.astype(BF16).astype(F32)
    return jnp.where(left_half(value.shape), high, value - high).astype(BF16)


def tiles(count, body, size=TILE):
    def step(index, carry):
        body(pl.ds(pl.multiple_of(index * size, size), size))
        return carry

    lax.fori_loop(0, count // size, step, 0)


def product(left, right):
    return jnp.dot(left, right, preferred_element_type=F32)


def wide_transform(high, low, value, result):
    def body(rows):
        first = product(high[rows, :], value[...])
        second = product(low[rows, :], value[:, :LANES])
        result[rows, :] = first[:, :LANES] + first[:, LANES:] + second

    tiles(result.shape[0], body, DOT_TILE)


def half_transform(high, low, value, result):
    def body(rows):
        total = product(high[rows, :], value[...]) + product(low[rows, :], value[...])
        result[rows, :] = total + turned(total)

    tiles(result.shape[0], body, DOT_TILE)


def moved(value, steps):
    if steps == 0:
        return value
    count = value.shape[0]
    row = lax.broadcasted_iota(jnp.int32, value.shape, 0)
    keep = (row >= steps) if steps > 0 else (row < count + steps)
    return jnp.where(keep, pltpu.roll(value, steps % count, 0), 0.0)


def block_kernel(
    inputs, gate, taps, filters, w_out_hbm, cot, fwd_high_hbm, fwd_low_hbm, inv_high_hbm, inv_low_hbm,
    output, grad_inputs, grad_gate, grad_filters, grad_taps, grad_wout,
    w_out, fwd_high, fwd_low, inv_high, inv_low, cot_all, cot_send, cot_cols, first_send, first_got,
    second_send, second_got, gated_all, own_got, third_send, third_got, gate_send, gate_got,
    taps_send, taps_got, part_send, part_got, wide_short, half_short, half_long, wide_long,
    spec, grad_spec, signal, mixing, table_sems, send_sems, recv_sems, chan_send_sems, chan_recv_sems,
):
    parts, rows = first_got.shape[0], first_got.shape[1]
    chans, cols = cot_all.shape[0], inputs.shape[1]
    tokens = parts * rows
    tap_count = taps.shape[0]
    me = lax.axis_index("seq")
    mine = lax.axis_index("chan")

    tables = [
        pltpu.make_async_copy(source, target, table_sems.at[index])
        for index, (source, target) in enumerate(
            [
                (w_out_hbm, w_out), (fwd_high_hbm, fwd_high), (fwd_low_hbm, fwd_low),
                (inv_high_hbm, inv_high), (inv_low_hbm, inv_low),
            ]
        )
    ]
    for table in tables:
        table.start()

    barrier = pltpu.get_barrier_semaphore()
    for step in range(1, parts):
        pl.semaphore_signal(
            barrier, inc=1, device_id=(lax.rem(me + step, parts), mine),
            device_id_type=pl.DeviceIdType.MESH,
        )
    for step in range(1, chans):
        pl.semaphore_signal(
            barrier, inc=1, device_id=(me, lax.rem(mine + step, chans)),
            device_id_type=pl.DeviceIdType.MESH,
        )
    pl.semaphore_wait(barrier, parts + chans - 2)

    def to_seq(kind, step, source, target):
        return pltpu.make_async_remote_copy(
            src_ref=source, dst_ref=target,
            send_sem=send_sems.at[kind, step], recv_sem=recv_sems.at[kind, step],
            device_id=(lax.rem(me + step, parts), mine), device_id_type=pl.DeviceIdType.MESH,
        )

    def to_chan(kind, step, source, target):
        return pltpu.make_async_remote_copy(
            src_ref=source, dst_ref=target,
            send_sem=chan_send_sems.at[kind, step], recv_sem=chan_recv_sems.at[kind, step],
            device_id=(me, lax.rem(mine + step, chans)), device_id_type=pl.DeviceIdType.MESH,
        )

    def launch(copies):
        for copy in copies:
            copy.start()
        return copies

    def arrive(copies):
        for copy in copies:
            copy.wait_recv()

    def exchange(kind, sent, got):
        copies = launch(
            [
                to_seq(kind, step, sent.at[lax.rem(me + step, parts)], got.at[me])
                for step in range(1, parts)
            ]
        )
        got[pl.ds(me, 1)] = sent[pl.ds(me, 1)]
        return copies

    def pack(left, right, target):
        for pair in range(parts // 2):
            span = slice(pair * LANES, (pair + 1) * LANES)
            a, b = (left[:, span].astype(F32), right[:, span].astype(F32))
            low = left_half(a.shape)
            target[2 * pair] = jnp.where(low, a, turned(b)).astype(BF16)
            target[2 * pair + 1] = jnp.where(low, turned(a), b).astype(BF16)

    cot_copies = launch([to_chan(0, step, cot, cot_all.at[mine]) for step in range(1, chans)])
    cot_all[pl.ds(mine, 1)] = cot[...][None]
    pack(inputs, filters, first_send)
    first_copies = exchange(0, first_send, first_got)

    own_taps = taps[:, pl.ds(pl.multiple_of(lax.div(me, 2) * LANES, LANES), LANES)]
    odd = jnp.full(own_taps.shape, lax.rem(me, 2), jnp.int32) == 1
    own_taps = jnp.where(odd, turned(own_taps), own_taps)
    tap_ids = lax.broadcasted_iota(jnp.int32, own_taps.shape, 0)
    mixing[...] = jnp.where(left_half(own_taps.shape), own_taps, (tap_ids == 0).astype(F32))

    arrive(first_copies)
    packed = first_got[...].reshape(tokens, LANES).astype(F32)
    mixed = packed * mixing[0:1, :]
    for tap in range(1, tap_count):
        mixed = mixed + mixing[tap : tap + 1, :] * moved(packed, tap)
    high, low = split_value(mixed)
    wide_short[:, :LANES] = high
    wide_short[:, LANES:] = low
    tables[1].wait()
    tables[2].wait()
    wide_transform(fwd_high, fwd_low, wide_short, spec)

    arrive(cot_copies)
    tables[0].wait()
    grad_gated = jnp.zeros((rows, cols), F32)
    for chan in range(chans):
        grad_gated = grad_gated + lax.dot_general(
            cot_all[chan], w_out[:, chan * cols : (chan + 1) * cols],
            (((1,), (1,)), ((), ())), preferred_element_type=F32,
        )
    pack(gate, grad_gated, second_send)
    second_copies = exchange(1, second_send, second_got)
    share = chans * cols // parts
    quarter_rows = rows // chans
    quarter = pl.ds(pl.multiple_of(mine * quarter_rows, quarter_rows), quarter_rows)
    for part in range(parts):
        chan, start = divmod(part * share, cols)
        cot_send[part] = cot_all[chan, quarter, start : start + share]
    cot_col_copies = launch(
        [
            to_seq(
                2, step, cot_send.at[lax.rem(me + step, parts)], cot_cols.at[me, quarter]
            )
            for step in range(1, parts)
        ]
    )
    cot_cols[pl.ds(me, 1), quarter] = cot_send[pl.ds(me, 1)]

    def multiply(rows_at):
        other = pl.ds(pl.multiple_of(rows_at.start + tokens, TILE), TILE)
        real, imag = (spec[rows_at, :], spec[other, :])
        real_turned, imag_turned = (turned(real), turned(imag))
        half_long[rows_at, :] = packed_split(real * real_turned - imag * imag_turned)
        half_long[other, :] = packed_split(real * imag_turned + imag * real_turned)

    tiles(tokens, multiply)
    tables[3].wait()
    tables[4].wait()
    half_transform(inv_high, inv_low, half_long, signal)

    arrive(cot_col_copies)
    cot_row_copies = launch(
        [
            to_chan(2, step, cot_cols.at[:, quarter], cot_cols.at[:, quarter])
            for step in range(1, chans)
        ]
    )
    arrive(second_copies)
    for part in range(parts):
        span = slice(part * rows, (part + 1) * rows)
        branch = second_got[part].astype(F32)
        scaled = branch * signal[span, :]
        gated_all[pl.ds(me, 1), :, span] = scaled.T[:HALF].astype(BF16)[None]
        gate_send[part] = jnp.where(
            left_half((rows // 2, LANES)), turned(scaled[: rows // 2]), scaled[rows // 2 :]
        ).astype(BF16)
        half_short[span, :] = packed_split(branch * turned(branch))

    own_copies = launch(
        [
            to_seq(
                7, step,
                gated_all.at[
                    me, :, pl.ds(pl.multiple_of(lax.rem(me + step, parts) * rows, rows), rows)
                ],
                own_got.at[me],
            )
            for step in range(1, parts)
        ]
    )
    here = pl.ds(pl.multiple_of(me * rows, rows), rows)
    own_got[pl.ds(me, 1)] = gated_all[pl.ds(me, 1), :, here]
    line = launch(
        [to_seq(3, step, gated_all.at[me], gated_all.at[me]) for step in range(2, parts, 2)]
    )
    partner = me + 1 - 2 * lax.rem(me, 2)

    def hand_on(step):
        source = lax.rem(me + parts - step, parts)
        return pltpu.make_async_remote_copy(
            src_ref=gated_all.at[source], dst_ref=gated_all.at[source],
            send_sem=send_sems.at[8, step], recv_sem=recv_sems.at[8, step],
            device_id=(partner, mine), device_id_type=pl.DeviceIdType.MESH,
        )

    handed = launch([hand_on(0)])
    gate_copies = exchange(4, gate_send, gate_got)

    half_transform(fwd_high, fwd_low, half_short, grad_spec)

    arrive(own_copies)
    own_gated = own_got[...].astype(F32).reshape(parts * HALF, rows).T.astype(BF16)
    for chan in range(chans):
        part_send[chan] = product(own_gated, w_out[:, chan * cols : (chan + 1) * cols]).astype(BF16)
    part_copies = launch(
        [
            to_chan(1, step, part_send.at[lax.rem(mine + step, chans)], part_got.at[mine])
            for step in range(1, chans)
        ]
    )
    part_got[pl.ds(mine, 1)] = part_send[pl.ds(mine, 1)]

    for step, copy in zip(range(2, parts, 2), line):
        copy.wait_recv()
        handed += launch([hand_on(step)])

    def back(rows_at):
        other = pl.ds(pl.multiple_of(rows_at.start + tokens, TILE), TILE)
        real, imag = (turned(spec[rows_at, :]), turned(spec[other, :]))
        grad_real, grad_imag = (grad_spec[rows_at, :], grad_spec[other, :])
        high, low = split_value(real * grad_real + imag * grad_imag)
        wide_long[rows_at, :LANES] = high
        wide_long[rows_at, LANES:] = low
        high, low = split_value(real * grad_imag - imag * grad_real)
        wide_long[other, :LANES] = high
        wide_long[other, LANES:] = low

    tiles(tokens, back)
    wide_transform(inv_high, inv_low, wide_long, signal)
    grads = signal[...]
    mixed_back = grads * mixing[0:1, :]
    packed = first_got[...].reshape(tokens, LANES).astype(F32)
    taps_send[...] = jnp.zeros_like(taps_send)
    for tap in range(tap_count):
        if tap:
            mixed_back = mixed_back + mixing[tap : tap + 1, :] * moved(grads, -tap)
        taps_send[tap : tap + 1, :] = jnp.sum(
            moved(packed, tap) * grads, axis=0, keepdims=True
        )
    third_send[...] = mixed_back.astype(BF16).reshape(parts, rows, LANES)
    third_copies = exchange(5, third_send, third_got)
    taps_copies = launch(
        [to_seq(6, step, taps_send, taps_got.at[me]) for step in range(1, parts)]
    )
    taps_got[pl.ds(me, 1)] = taps_send[...][None]

    arrive(cot_row_copies)
    arrive(handed)
    grad_wout[...] = product(
        gated_all[...].reshape(parts * HALF, tokens), cot_cols[...].reshape(tokens, share)
    )
    arrive(gate_copies)
    arrive(third_copies)
    arrive(taps_copies)
    for pair in range(parts // 2):
        span = slice(pair * LANES, (pair + 1) * LANES)
        a, b = (third_got[2 * pair].astype(F32), third_got[2 * pair + 1].astype(F32))
        low = left_half(a.shape)
        grad_inputs[:, span] = jnp.where(low, a, turned(b)).astype(BF16)
        grad_filters[:, span] = jnp.where(low, turned(a), b)
        a, b = (gate_got[2 * pair].astype(F32), gate_got[2 * pair + 1].astype(F32))
        low = left_half(a.shape)
        grad_gate[: rows // 2, span] = jnp.where(low, a, turned(b)).astype(BF16)
        grad_gate[rows // 2 :, span] = jnp.where(low, turned(a), b).astype(BF16)
        a, b = (taps_got[2 * pair], taps_got[2 * pair + 1])
        grad_taps[:, span] = jnp.where(left_half(a.shape), a, turned(b))[:tap_count]

    arrive(part_copies)
    total = part_got[0].astype(F32)
    for chan in range(1, chans):
        total = total + part_got[chan].astype(F32)
    output[...] = total.astype(BF16)
    for copies in (
        cot_copies, first_copies, second_copies, cot_col_copies, cot_row_copies, own_copies, line,
        handed, gate_copies, third_copies, taps_copies, part_copies,
    ):
        for copy in copies:
            copy.wait_send()


def store_kernel(*refs):
    count = len(refs) // 2
    for source, target in zip(refs[:count], refs[count:]):
        target[...] = source[...]


def dense_local(inputs, gate_branch, short_taps, filters, w_out, cotangent):
    parts = lax.axis_size("seq")
    chans = lax.axis_size("chan")
    rows, cols = inputs.shape
    tokens = rows * parts
    share = cols * chans // parts
    tap_rows = 8
    (fwd_high, fwd_low), (inv_high, inv_low) = dense_tables(tokens)
    vmem = pl.BlockSpec(memory_space=pltpu.VMEM)
    hbm = pl.BlockSpec(memory_space=pl.ANY)
    shape = jax.ShapeDtypeStruct
    results = pl.pallas_call(
        block_kernel,
        out_shape=(
            shape((rows, cols), BF16), shape((rows, cols), BF16), shape((rows, cols), BF16),
            shape((rows, cols), F32), shape(short_taps.shape, F32), shape((cols, share), F32),
        ),
        in_specs=[vmem] * 4 + [hbm, vmem] + [hbm] * 4,
        out_specs=[vmem] * 6,
        scratch_shapes=[
            pltpu.VMEM(w_out.shape, BF16),
            pltpu.VMEM((2 * tokens, tokens), BF16), pltpu.VMEM((2 * tokens, tokens), BF16),
            pltpu.VMEM((tokens, 2 * tokens), BF16), pltpu.VMEM((tokens, 2 * tokens), BF16),
            pltpu.VMEM((chans, rows, cols), BF16),
            pltpu.VMEM((parts, rows // chans, share), BF16), pltpu.VMEM((parts, rows, share), BF16),
            pltpu.VMEM((parts, rows, LANES), BF16), pltpu.VMEM((parts, rows, LANES), BF16),
            pltpu.VMEM((parts, rows, LANES), BF16), pltpu.VMEM((parts, rows, LANES), BF16),
            pltpu.VMEM((parts, HALF, tokens), BF16), pltpu.VMEM((parts, HALF, rows), BF16),
            pltpu.VMEM((parts, rows, LANES), BF16), pltpu.VMEM((parts, rows, LANES), BF16),
            pltpu.VMEM((parts, rows // 2, LANES), BF16), pltpu.VMEM((parts, rows // 2, LANES), BF16),
            pltpu.VMEM((tap_rows, LANES), F32), pltpu.VMEM((parts, tap_rows, LANES), F32),
            pltpu.VMEM((chans, rows, cols), BF16), pltpu.VMEM((chans, rows, cols), BF16),
            pltpu.VMEM((tokens, 2 * LANES), BF16), pltpu.VMEM((tokens, LANES), BF16),
            pltpu.VMEM((2 * tokens, LANES), BF16), pltpu.VMEM((2 * tokens, 2 * LANES), BF16),
            pltpu.VMEM((2 * tokens, LANES), F32), pltpu.VMEM((2 * tokens, LANES), F32),
            pltpu.VMEM((tokens, LANES), F32), pltpu.VMEM((short_taps.shape[0], LANES), F32),
            pltpu.SemaphoreType.DMA((5,)),
            pltpu.SemaphoreType.DMA((9, parts)), pltpu.SemaphoreType.DMA((9, parts)),
            pltpu.SemaphoreType.DMA((3, chans)), pltpu.SemaphoreType.DMA((3, chans)),
        ],
        compiler_params=pltpu.CompilerParams(
            collective_id=0, has_side_effects=True, vmem_limit_bytes=56 * 1024 * 1024
        ),
    )(inputs, gate_branch, short_taps, filters, w_out, cotangent, fwd_high, fwd_low, inv_high, inv_low)
    count = len(results)
    return pl.pallas_call(
        store_kernel,
        out_shape=[shape(value.shape, value.dtype) for value in results],
        in_specs=[vmem] * count,
        out_specs=[vmem] * count,
    )(*results)


def local(inputs, *others):
    parts = lax.axis_size("seq")
    rows, cols = inputs.shape
    fits = rows * parts <= DENSE_TOKENS and rows % LANES == 0 and parts % 2 == 0
    fits = fits and cols == HALF * parts and rows % (16 * lax.axis_size("chan")) == 0
    return (dense_local if fits else panel_local)(inputs, *others)


def solution(mesh):
    in_specs = (
        P("seq", "chan"),
        P("seq", "chan"),
        P(None, "chan"),
        P("seq", "chan"),
        P("chan", None),
        P("seq", "chan"),
    )
    out_specs = (
        P("seq", "chan"),
        P("seq", "chan"),
        P("seq", "chan"),
        P("seq", "chan"),
        P(None, "chan"),
        P("chan", "seq"),
    )
    return jax.shard_map(local, mesh=mesh, in_specs=in_specs, out_specs=out_specs, check_vma=False)
```

```python
import math

import functools

import jax
import jax.numpy as jnp
import numpy as np
from jax import lax
from jax.experimental import pallas as pl
from jax.experimental.pallas import tpu as pltpu
from jax.sharding import PartitionSpec as P

HIGHEST = lax.Precision.HIGHEST


def from_behind(value, axis, steps):
    count = lax.axis_size(axis)
    first, last = (max(0, -steps), min(count, count - steps))
    return lax.ppermute(value, axis, [(source, source + steps) for source in range(first, last)])


def angle_table(row_len, col_len, modulus, row_start, col_start, direction):
    row_ids = lax.iota(jnp.int32, row_len)[:, None] + row_start
    col_ids = lax.iota(jnp.int32, col_len)[None, :] + col_start
    phase = row_ids * col_ids % modulus
    angles = phase.astype(jnp.float32) * (direction * 2.0 * math.pi / modulus)
    return (jnp.cos(angles), jnp.sin(angles))


def column_dft(real_part, imag_part, length, form, direction):
    cos_table, sin_table = angle_table(length, length, length, 0, 0, direction)
    new_real = jnp.einsum(form, real_part, cos_table, precision=HIGHEST) - jnp.einsum(
        form, imag_part, sin_table, precision=HIGHEST
    )
    new_imag = jnp.einsum(form, real_part, sin_table, precision=HIGHEST) + jnp.einsum(
        form, imag_part, cos_table, precision=HIGHEST
    )
    return (new_real, new_imag)


def panel_forward(signal):
    stack_size = signal.shape[0]
    block_len = signal.shape[1]
    part_count = lax.axis_size("seq")
    my_index = lax.axis_index("seq")
    narrow = block_len // part_count
    row_order = 2 * part_count
    full_len = row_order * block_len
    by_column = lax.all_to_all(signal[:, None], "seq", split_axis=2, concat_axis=1, tiled=True)
    row_cos, row_sin = angle_table(row_order, part_count, row_order, 0, 0, -1.0)
    real_part = jnp.einsum("ja,kabf->kjbf", row_cos, by_column, precision=HIGHEST)
    imag_part = jnp.einsum("ja,kabf->kjbf", row_sin, by_column, precision=HIGHEST)
    twist_cos, twist_sin = angle_table(row_order, narrow, full_len, 0, my_index * narrow, -1.0)
    twist_cos = twist_cos[None, :, :, None]
    twist_sin = twist_sin[None, :, :, None]
    real_twist = real_part * twist_cos - imag_part * twist_sin
    imag_twist = real_part * twist_sin + imag_part * twist_cos
    by_rows = lax.all_to_all(
        jnp.concatenate([real_twist, imag_twist], 0), "seq", split_axis=1, concat_axis=2, tiled=True
    )
    return column_dft(by_rows[:stack_size], by_rows[stack_size:], block_len, "kjbf,bm->kjmf", -1.0)


def panel_inverse(real_part, imag_part):
    stack_size = real_part.shape[0]
    block_len = real_part.shape[2]
    part_count = lax.axis_size("seq")
    my_index = lax.axis_index("seq")
    row_order = 2 * part_count
    full_len = row_order * block_len
    real_back, imag_back = column_dft(real_part, imag_part, block_len, "kjmf,mb->kjbf", 1.0)
    twist_cos, twist_sin = angle_table(2, block_len, full_len, my_index * 2, 0, 1.0)
    twist_cos = twist_cos[None, :, :, None]
    twist_sin = twist_sin[None, :, :, None]
    real_twist = (real_back * twist_cos - imag_back * twist_sin) / block_len
    imag_twist = (real_back * twist_sin + imag_back * twist_cos) / block_len
    by_column = lax.all_to_all(
        jnp.concatenate([real_twist, imag_twist], 0), "seq", split_axis=2, concat_axis=1, tiled=True
    )
    row_cos, row_sin = angle_table(part_count, row_order, row_order, 0, 0, 1.0)
    signal = (
        jnp.einsum("aj,kjbf->kabf", row_cos, by_column[:stack_size], precision=HIGHEST)
        - jnp.einsum("aj,kjbf->kabf", row_sin, by_column[stack_size:], precision=HIGHEST)
    ) / row_order
    returned = lax.all_to_all(signal, "seq", split_axis=1, concat_axis=2, tiled=True)
    return returned[:, 0]


def panel_local(inputs, gate_branch, short_taps, filters, w_out, cotangent):
    forward_fn, inverse_fn = (panel_forward, panel_inverse)
    tap_count = short_taps.shape[0]
    row_count = inputs.shape[0]
    left_tail = from_behind(inputs[row_count - (tap_count - 1) :], "seq", 1)
    extended = jnp.concatenate([left_tail, inputs], 0).astype(jnp.float32)
    mixed = jnp.zeros((row_count, inputs.shape[1]), jnp.float32)
    for tap_index in range(tap_count):
        start_row = tap_count - 1 - tap_index
        mixed = mixed + short_taps[tap_index] * extended[start_row : start_row + row_count]
    spec_real, spec_imag = forward_fn(jnp.stack([mixed, filters], 0))
    mixed_real, filter_real = (spec_real[0], spec_real[1])
    mixed_imag, filter_imag = (spec_imag[0], spec_imag[1])
    prod_real = mixed_real * filter_real - mixed_imag * filter_imag
    prod_imag = mixed_real * filter_imag + mixed_imag * filter_real
    convolved = inverse_fn(prod_real[None], prod_imag[None])[0]
    gate_wide = gate_branch.astype(jnp.float32)
    gated = (gate_wide * convolved).astype(jnp.bfloat16)
    out_terms = jnp.dot(gated, w_out, preferred_element_type=jnp.float32)
    output = lax.psum_scatter(out_terms, "chan", scatter_dimension=1, tiled=True).astype(
        jnp.bfloat16
    )
    full_cot = lax.all_gather(cotangent, "chan", axis=1, tiled=True)
    grad_gated = lax.dot_general(
        full_cot, w_out, (((1,), (1,)), ((), ())), preferred_element_type=jnp.float32
    )
    grad_gate = (grad_gated * convolved).astype(jnp.bfloat16)
    grad_conv = grad_gated * gate_wide
    grad_real, grad_imag = forward_fn(grad_conv[None])
    grad_real = grad_real[0]
    grad_imag = grad_imag[0]
    back_real = jnp.stack(
        [
            filter_real * grad_real + filter_imag * grad_imag,
            mixed_real * grad_real + mixed_imag * grad_imag,
        ],
        0,
    )
    back_imag = jnp.stack(
        [
            filter_real * grad_imag - filter_imag * grad_real,
            mixed_real * grad_imag - mixed_imag * grad_real,
        ],
        0,
    )
    gradients = inverse_fn(back_real, back_imag)
    grad_mixed = gradients[0]
    grad_filters = gradients[1]
    right_head = from_behind(grad_mixed[: tap_count - 1], "seq", -1)
    grad_ext = jnp.concatenate([grad_mixed, right_head], 0)
    grad_wide = jnp.zeros_like(grad_mixed)
    tap_rows = []
    for tap_index in range(tap_count):
        start_row = tap_count - 1 - tap_index
        grad_wide = grad_wide + short_taps[tap_index] * grad_ext[tap_index : tap_index + row_count]
        tap_rows.append(jnp.sum(extended[start_row : start_row + row_count] * grad_mixed, axis=0))
    grad_inputs = grad_wide.astype(jnp.bfloat16)
    grad_taps = lax.psum(jnp.stack(tap_rows, 0), "seq")
    weight_terms = lax.dot_general(
        gated, full_cot, (((0,), (0,)), ((), ())), preferred_element_type=jnp.float32
    )
    grad_wout = lax.psum_scatter(weight_terms, "seq", scatter_dimension=1, tiled=True)
    return (output, grad_inputs, grad_gate, grad_filters, grad_taps, grad_wout)


DENSE_TOKENS = 2048


def split_table(table):
    high = table.astype(jnp.bfloat16)
    low = (table - high.astype(np.float64)).astype(jnp.bfloat16)
    return (high, low)


def dense_tables(tokens):
    freq = np.arange(tokens, dtype=np.int64)[:, None]
    time = np.arange(tokens, dtype=np.int64)[None, :]
    angles = ((2 * freq + 1) * time % (4 * tokens)) * (2.0 * np.pi / (4 * tokens))
    forward = np.concatenate([np.cos(angles), -np.sin(angles)], 0)
    inverse = forward.T / tokens
    return (split_table(forward), split_table(inverse))


LANES = 128
HALF = 64
TILE = 256
DOT_TILE = 512
BF16 = jnp.bfloat16
F32 = jnp.float32


def left_half(shape):
    return lax.broadcasted_iota(jnp.int32, shape, 1) < HALF


def turned(value):
    return pltpu.roll(value, HALF, 1)


def split_value(value):
    high = value.astype(BF16)
    return (high, (value - high.astype(F32)).astype(BF16))


def packed_split(value):
    high = value.astype(BF16).astype(F32)
    return jnp.where(left_half(value.shape), high, value - high).astype(BF16)


def tiles(count, body, size=TILE):
    def step(index, carry):
        body(pl.ds(pl.multiple_of(index * size, size), size))
        return carry

    lax.fori_loop(0, count // size, step, 0)


def product(left, right):
    return jnp.dot(left, right, preferred_element_type=F32)


def wide_transform(high, low, value, result):
    def body(rows):
        first = product(high[rows, :], value[...])
        second = product(low[rows, :], value[:, :LANES])
        result[rows, :] = first[:, :LANES] + first[:, LANES:] + second

    tiles(result.shape[0], body, DOT_TILE)


def half_transform(high, low, value, result):
    def body(rows):
        total = product(high[rows, :], value[...]) + product(low[rows, :], value[...])
        result[rows, :] = total + turned(total)

    tiles(result.shape[0], body, DOT_TILE)


def moved(value, steps):
    if steps == 0:
        return value
    count = value.shape[0]
    row = lax.broadcasted_iota(jnp.int32, value.shape, 0)
    keep = (row >= steps) if steps > 0 else (row < count + steps)
    return jnp.where(keep, pltpu.roll(value, steps % count, 0), 0.0)


def block_kernel(
    inputs, gate, taps, filters, w_out_hbm, cot, fwd_high_hbm, fwd_low_hbm, inv_high_hbm, inv_low_hbm,
    output, grad_inputs, grad_gate, grad_filters, grad_taps, grad_wout,
    w_out, fwd_high, fwd_low, inv_high, inv_low, cot_all, cot_send, cot_cols, first_send, first_got,
    second_send, second_got, gated_all, own_got, third_send, third_got, gate_send, gate_got,
    taps_send, taps_got, part_send, part_got, wide_short, half_short, half_long, wide_long,
    spec, grad_spec, signal, mixing, table_sems, send_sems, recv_sems, chan_send_sems, chan_recv_sems,
):
    parts, rows = first_got.shape[0], first_got.shape[1]
    chans, cols = cot_all.shape[0], inputs.shape[1]
    tokens = parts * rows
    tap_count = taps.shape[0]
    me = lax.axis_index("seq")
    mine = lax.axis_index("chan")

    tables = [
        pltpu.make_async_copy(source, target, table_sems.at[index])
        for index, (source, target) in enumerate(
            [
                (w_out_hbm, w_out), (fwd_high_hbm, fwd_high), (fwd_low_hbm, fwd_low),
                (inv_high_hbm, inv_high), (inv_low_hbm, inv_low),
            ]
        )
    ]
    for table in tables:
        table.start()

    barrier = pltpu.get_barrier_semaphore()
    for step in range(1, parts):
        pl.semaphore_signal(
            barrier, inc=1, device_id=(lax.rem(me + step, parts), mine),
            device_id_type=pl.DeviceIdType.MESH,
        )
    for step in range(1, chans):
        pl.semaphore_signal(
            barrier, inc=1, device_id=(me, lax.rem(mine + step, chans)),
            device_id_type=pl.DeviceIdType.MESH,
        )
    pl.semaphore_wait(barrier, parts + chans - 2)

    def to_seq(kind, step, source, target):
        return pltpu.make_async_remote_copy(
            src_ref=source, dst_ref=target,
            send_sem=send_sems.at[kind, step], recv_sem=recv_sems.at[kind, step],
            device_id=(lax.rem(me + step, parts), mine), device_id_type=pl.DeviceIdType.MESH,
        )

    def to_chan(kind, step, source, target):
        return pltpu.make_async_remote_copy(
            src_ref=source, dst_ref=target,
            send_sem=chan_send_sems.at[kind, step], recv_sem=chan_recv_sems.at[kind, step],
            device_id=(me, lax.rem(mine + step, chans)), device_id_type=pl.DeviceIdType.MESH,
        )

    def launch(copies):
        for copy in copies:
            copy.start()
        return copies

    def arrive(copies):
        for copy in copies:
            copy.wait_recv()

    def exchange(kind, sent, got):
        copies = launch(
            [
                to_seq(kind, step, sent.at[lax.rem(me + step, parts)], got.at[me])
                for step in range(1, parts)
            ]
        )
        got[pl.ds(me, 1)] = sent[pl.ds(me, 1)]
        return copies

    def pack(left, right, target):
        for pair in range(parts // 2):
            span = slice(pair * LANES, (pair + 1) * LANES)
            a, b = (left[:, span].astype(F32), right[:, span].astype(F32))
            low = left_half(a.shape)
            target[2 * pair] = jnp.where(low, a, turned(b)).astype(BF16)
            target[2 * pair + 1] = jnp.where(low, turned(a), b).astype(BF16)

    cot_copies = launch([to_chan(0, step, cot, cot_all.at[mine]) for step in range(1, chans)])
    cot_all[pl.ds(mine, 1)] = cot[...][None]
    pack(inputs, filters, first_send)
    first_copies = exchange(0, first_send, first_got)

    own_taps = taps[:, pl.ds(pl.multiple_of(lax.div(me, 2) * LANES, LANES), LANES)]
    odd = jnp.full(own_taps.shape, lax.rem(me, 2), jnp.int32) == 1
    own_taps = jnp.where(odd, turned(own_taps), own_taps)
    tap_ids = lax.broadcasted_iota(jnp.int32, own_taps.shape, 0)
    mixing[...] = jnp.where(left_half(own_taps.shape), own_taps, (tap_ids == 0).astype(F32))

    arrive(first_copies)
    packed = first_got[...].reshape(tokens, LANES).astype(F32)
    mixed = packed * mixing[0:1, :]
    for tap in range(1, tap_count):
        mixed = mixed + mixing[tap : tap + 1, :] * moved(packed, tap)
    high, low = split_value(mixed)
    wide_short[:, :LANES] = high
    wide_short[:, LANES:] = low
    tables[1].wait()
    tables[2].wait()
    wide_transform(fwd_high, fwd_low, wide_short, spec)

    arrive(cot_copies)
    tables[0].wait()
    grad_gated = jnp.zeros((rows, cols), F32)
    for chan in range(chans):
        grad_gated = grad_gated + lax.dot_general(
            cot_all[chan], w_out[:, chan * cols : (chan + 1) * cols],
            (((1,), (1,)), ((), ())), preferred_element_type=F32,
        )
    pack(gate, grad_gated, second_send)
    second_copies = exchange(1, second_send, second_got)
    share = chans * cols // parts
    quarter_rows = rows // chans
    quarter = pl.ds(pl.multiple_of(mine * quarter_rows, quarter_rows), quarter_rows)
    for part in range(parts):
        chan, start = divmod(part * share, cols)
        cot_send[part] = cot_all[chan, quarter, start : start + share]
    cot_col_copies = launch(
        [
            to_seq(
                2, step, cot_send.at[lax.rem(me + step, parts)], cot_cols.at[me, quarter]
            )
            for step in range(1, parts)
        ]
    )
    cot_cols[pl.ds(me, 1), quarter] = cot_send[pl.ds(me, 1)]

    def multiply(rows_at):
        other = pl.ds(pl.multiple_of(rows_at.start + tokens, TILE), TILE)
        real, imag = (spec[rows_at, :], spec[other, :])
        real_turned, imag_turned = (turned(real), turned(imag))
        half_long[rows_at, :] = packed_split(real * real_turned - imag * imag_turned)
        half_long[other, :] = packed_split(real * imag_turned + imag * real_turned)

    tiles(tokens, multiply)
    tables[3].wait()
    tables[4].wait()
    half_transform(inv_high, inv_low, half_long, signal)

    arrive(cot_col_copies)
    cot_row_copies = launch(
        [
            to_chan(2, step, cot_cols.at[:, quarter], cot_cols.at[:, quarter])
            for step in range(1, chans)
        ]
    )
    arrive(second_copies)
    for part in range(parts):
        span = slice(part * rows, (part + 1) * rows)
        branch = second_got[part].astype(F32)
        scaled = branch * signal[span, :]
        gated_all[pl.ds(me, 1), :, span] = scaled.T[:HALF].astype(BF16)[None]
        gate_send[part] = jnp.where(
            left_half((rows // 2, LANES)), turned(scaled[: rows // 2]), scaled[rows // 2 :]
        ).astype(BF16)
        half_short[span, :] = packed_split(branch * turned(branch))

    own_copies = launch(
        [
            to_seq(
                7, step,
                gated_all.at[
                    me, :, pl.ds(pl.multiple_of(lax.rem(me + step, parts) * rows, rows), rows)
                ],
                own_got.at[me],
            )
            for step in range(1, parts)
        ]
    )
    here = pl.ds(pl.multiple_of(me * rows, rows), rows)
    own_got[pl.ds(me, 1)] = gated_all[pl.ds(me, 1), :, here]
    line = [
        launch(
            [
                to_seq(kind, step, gated_all.at[me, span], gated_all.at[me, span])
                for step in range(2, parts, 2)
            ]
        )
        for kind, span in ((3, slice(0, HALF // 2)), (9, slice(HALF // 2, HALF)))
    ]
    partner = me + 1 - 2 * lax.rem(me, 2)

    def hand_on(kind, step, span):
        source = lax.rem(me + parts - step, parts)
        return pltpu.make_async_remote_copy(
            src_ref=gated_all.at[source, span], dst_ref=gated_all.at[source, span],
            send_sem=send_sems.at[kind, step], recv_sem=recv_sems.at[kind, step],
            device_id=(partner, mine), device_id_type=pl.DeviceIdType.MESH,
        )

    handed = launch([hand_on(8, 0, slice(0, HALF))])

    half_transform(fwd_high, fwd_low, half_short, grad_spec)

    arrive(own_copies)
    own_gated = own_got[...].astype(F32).reshape(parts * HALF, rows).T.astype(BF16)
    for chan in range(chans):
        part_send[chan] = product(own_gated, w_out[:, chan * cols : (chan + 1) * cols]).astype(BF16)
    part_copies = launch(
        [
            to_chan(1, step, part_send.at[lax.rem(mine + step, chans)], part_got.at[mine])
            for step in range(1, chans)
        ]
    )
    part_got[pl.ds(mine, 1)] = part_send[pl.ds(mine, 1)]

    for step, copy in zip(range(2, parts, 2), line[0]):
        copy.wait_recv()
        handed += launch([hand_on(8, step, slice(0, HALF // 2))])
    gate_copies = exchange(4, gate_send, gate_got)

    def back(rows_at):
        other = pl.ds(pl.multiple_of(rows_at.start + tokens, TILE), TILE)
        real, imag = (turned(spec[rows_at, :]), turned(spec[other, :]))
        grad_real, grad_imag = (grad_spec[rows_at, :], grad_spec[other, :])
        high, low = split_value(real * grad_real + imag * grad_imag)
        wide_long[rows_at, :LANES] = high
        wide_long[rows_at, LANES:] = low
        high, low = split_value(real * grad_imag - imag * grad_real)
        wide_long[other, :LANES] = high
        wide_long[other, LANES:] = low

    tiles(tokens, back)
    wide_transform(inv_high, inv_low, wide_long, signal)
    for step, copy in zip(range(2, parts, 2), line[1]):
        copy.wait_recv()
        handed += launch([hand_on(10, step, slice(HALF // 2, HALF))])
    grads = signal[...]
    mixed_back = grads * mixing[0:1, :]
    packed = first_got[...].reshape(tokens, LANES).astype(F32)
    taps_send[...] = jnp.zeros_like(taps_send)
    for tap in range(tap_count):
        if tap:
            mixed_back = mixed_back + mixing[tap : tap + 1, :] * moved(grads, -tap)
        taps_send[tap : tap + 1, :] = jnp.sum(
            moved(packed, tap) * grads, axis=0, keepdims=True
        )
    third_send[...] = mixed_back.astype(BF16).reshape(parts, rows, LANES)
    third_copies = exchange(5, third_send, third_got)
    taps_copies = launch(
        [to_seq(6, step, taps_send, taps_got.at[me]) for step in range(1, parts)]
    )
    taps_got[pl.ds(me, 1)] = taps_send[...][None]

    arrive(cot_row_copies)
    arrive(handed)
    grad_wout[...] = product(
        gated_all[...].reshape(parts * HALF, tokens), cot_cols[...].reshape(tokens, share)
    )
    arrive(gate_copies)
    arrive(third_copies)
    arrive(taps_copies)
    for pair in range(parts // 2):
        span = slice(pair * LANES, (pair + 1) * LANES)
        a, b = (third_got[2 * pair].astype(F32), third_got[2 * pair + 1].astype(F32))
        low = left_half(a.shape)
        grad_inputs[:, span] = jnp.where(low, a, turned(b)).astype(BF16)
        grad_filters[:, span] = jnp.where(low, turned(a), b)
        a, b = (gate_got[2 * pair].astype(F32), gate_got[2 * pair + 1].astype(F32))
        low = left_half(a.shape)
        grad_gate[: rows // 2, span] = jnp.where(low, a, turned(b)).astype(BF16)
        grad_gate[rows // 2 :, span] = jnp.where(low, turned(a), b).astype(BF16)
        a, b = (taps_got[2 * pair], taps_got[2 * pair + 1])
        grad_taps[:, span] = jnp.where(left_half(a.shape), a, turned(b))[:tap_count]

    arrive(part_copies)
    total = part_got[0].astype(F32)
    for chan in range(1, chans):
        total = total + part_got[chan].astype(F32)
    output[...] = total.astype(BF16)
    for copies in (
        cot_copies, first_copies, second_copies, cot_col_copies, cot_row_copies, own_copies, *line,
        handed, gate_copies, third_copies, taps_copies, part_copies,
    ):
        for copy in copies:
            copy.wait_send()


def store_kernel(*refs):
    count = len(refs) // 2
    for source, target in zip(refs[:count], refs[count:]):
        target[...] = source[...]


def dense_local(inputs, gate_branch, short_taps, filters, w_out, cotangent):
    parts = lax.axis_size("seq")
    chans = lax.axis_size("chan")
    rows, cols = inputs.shape
    tokens = rows * parts
    share = cols * chans // parts
    tap_rows = 8
    (fwd_high, fwd_low), (inv_high, inv_low) = dense_tables(tokens)
    vmem = pl.BlockSpec(memory_space=pltpu.VMEM)
    hbm = pl.BlockSpec(memory_space=pl.ANY)
    shape = jax.ShapeDtypeStruct
    results = pl.pallas_call(
        block_kernel,
        out_shape=(
            shape((rows, cols), BF16), shape((rows, cols), BF16), shape((rows, cols), BF16),
            shape((rows, cols), F32), shape(short_taps.shape, F32), shape((cols, share), F32),
        ),
        in_specs=[vmem] * 4 + [hbm, vmem] + [hbm] * 4,
        out_specs=[vmem] * 6,
        scratch_shapes=[
            pltpu.VMEM(w_out.shape, BF16),
            pltpu.VMEM((2 * tokens, tokens), BF16), pltpu.VMEM((2 * tokens, tokens), BF16),
            pltpu.VMEM((tokens, 2 * tokens), BF16), pltpu.VMEM((tokens, 2 * tokens), BF16),
            pltpu.VMEM((chans, rows, cols), BF16),
            pltpu.VMEM((parts, rows // chans, share), BF16), pltpu.VMEM((parts, rows, share), BF16),
            pltpu.VMEM((parts, rows, LANES), BF16), pltpu.VMEM((parts, rows, LANES), BF16),
            pltpu.VMEM((parts, rows, LANES), BF16), pltpu.VMEM((parts, rows, LANES), BF16),
            pltpu.VMEM((parts, HALF, tokens), BF16), pltpu.VMEM((parts, HALF, rows), BF16),
            pltpu.VMEM((parts, rows, LANES), BF16), pltpu.VMEM((parts, rows, LANES), BF16),
            pltpu.VMEM((parts, rows // 2, LANES), BF16), pltpu.VMEM((parts, rows // 2, LANES), BF16),
            pltpu.VMEM((tap_rows, LANES), F32), pltpu.VMEM((parts, tap_rows, LANES), F32),
            pltpu.VMEM((chans, rows, cols), BF16), pltpu.VMEM((chans, rows, cols), BF16),
            pltpu.VMEM((tokens, 2 * LANES), BF16), pltpu.VMEM((tokens, LANES), BF16),
            pltpu.VMEM((2 * tokens, LANES), BF16), pltpu.VMEM((2 * tokens, 2 * LANES), BF16),
            pltpu.VMEM((2 * tokens, LANES), F32), pltpu.VMEM((2 * tokens, LANES), F32),
            pltpu.VMEM((tokens, LANES), F32), pltpu.VMEM((short_taps.shape[0], LANES), F32),
            pltpu.SemaphoreType.DMA((5,)),
            pltpu.SemaphoreType.DMA((11, parts)), pltpu.SemaphoreType.DMA((11, parts)),
            pltpu.SemaphoreType.DMA((3, chans)), pltpu.SemaphoreType.DMA((3, chans)),
        ],
        compiler_params=pltpu.CompilerParams(
            collective_id=0, has_side_effects=True, vmem_limit_bytes=56 * 1024 * 1024
        ),
    )(inputs, gate_branch, short_taps, filters, w_out, cotangent, fwd_high, fwd_low, inv_high, inv_low)
    count = len(results)
    return pl.pallas_call(
        store_kernel,
        out_shape=[shape(value.shape, value.dtype) for value in results],
        in_specs=[vmem] * count,
        out_specs=[vmem] * count,
    )(*results)


def local(inputs, *others):
    parts = lax.axis_size("seq")
    rows, cols = inputs.shape
    fits = rows * parts <= DENSE_TOKENS and rows % LANES == 0 and parts % 2 == 0
    fits = fits and cols == HALF * parts and rows % (16 * lax.axis_size("chan")) == 0
    return (dense_local if fits else panel_local)(inputs, *others)


def solution(mesh):
    in_specs = (
        P("seq", "chan"),
        P("seq", "chan"),
        P(None, "chan"),
        P("seq", "chan"),
        P("chan", None),
        P("seq", "chan"),
    )
    out_specs = (
        P("seq", "chan"),
        P("seq", "chan"),
        P("seq", "chan"),
        P("seq", "chan"),
        P(None, "chan"),
        P("chan", "seq"),
    )
    return jax.shard_map(local, mesh=mesh, in_specs=in_specs, out_specs=out_specs, check_vma=False)
```

```python
import math

import functools

import jax
import jax.numpy as jnp
import numpy as np
from jax import lax
from jax.experimental import pallas as pl
from jax.experimental.pallas import tpu as pltpu
from jax.sharding import PartitionSpec as P

HIGHEST = lax.Precision.HIGHEST


def from_behind(value, axis, steps):
    count = lax.axis_size(axis)
    first, last = (max(0, -steps), min(count, count - steps))
    return lax.ppermute(value, axis, [(source, source + steps) for source in range(first, last)])


def angle_table(row_len, col_len, modulus, row_start, col_start, direction):
    row_ids = lax.iota(jnp.int32, row_len)[:, None] + row_start
    col_ids = lax.iota(jnp.int32, col_len)[None, :] + col_start
    phase = row_ids * col_ids % modulus
    angles = phase.astype(jnp.float32) * (direction * 2.0 * math.pi / modulus)
    return (jnp.cos(angles), jnp.sin(angles))


def column_dft(real_part, imag_part, length, form, direction):
    cos_table, sin_table = angle_table(length, length, length, 0, 0, direction)
    new_real = jnp.einsum(form, real_part, cos_table, precision=HIGHEST) - jnp.einsum(
        form, imag_part, sin_table, precision=HIGHEST
    )
    new_imag = jnp.einsum(form, real_part, sin_table, precision=HIGHEST) + jnp.einsum(
        form, imag_part, cos_table, precision=HIGHEST
    )
    return (new_real, new_imag)


def panel_forward(signal):
    stack_size = signal.shape[0]
    block_len = signal.shape[1]
    part_count = lax.axis_size("seq")
    my_index = lax.axis_index("seq")
    narrow = block_len // part_count
    row_order = 2 * part_count
    full_len = row_order * block_len
    by_column = lax.all_to_all(signal[:, None], "seq", split_axis=2, concat_axis=1, tiled=True)
    row_cos, row_sin = angle_table(row_order, part_count, row_order, 0, 0, -1.0)
    real_part = jnp.einsum("ja,kabf->kjbf", row_cos, by_column, precision=HIGHEST)
    imag_part = jnp.einsum("ja,kabf->kjbf", row_sin, by_column, precision=HIGHEST)
    twist_cos, twist_sin = angle_table(row_order, narrow, full_len, 0, my_index * narrow, -1.0)
    twist_cos = twist_cos[None, :, :, None]
    twist_sin = twist_sin[None, :, :, None]
    real_twist = real_part * twist_cos - imag_part * twist_sin
    imag_twist = real_part * twist_sin + imag_part * twist_cos
    by_rows = lax.all_to_all(
        jnp.concatenate([real_twist, imag_twist], 0), "seq", split_axis=1, concat_axis=2, tiled=True
    )
    return column_dft(by_rows[:stack_size], by_rows[stack_size:], block_len, "kjbf,bm->kjmf", -1.0)


def panel_inverse(real_part, imag_part):
    stack_size = real_part.shape[0]
    block_len = real_part.shape[2]
    part_count = lax.axis_size("seq")
    my_index = lax.axis_index("seq")
    row_order = 2 * part_count
    full_len = row_order * block_len
    real_back, imag_back = column_dft(real_part, imag_part, block_len, "kjmf,mb->kjbf", 1.0)
    twist_cos, twist_sin = angle_table(2, block_len, full_len, my_index * 2, 0, 1.0)
    twist_cos = twist_cos[None, :, :, None]
    twist_sin = twist_sin[None, :, :, None]
    real_twist = (real_back * twist_cos - imag_back * twist_sin) / block_len
    imag_twist = (real_back * twist_sin + imag_back * twist_cos) / block_len
    by_column = lax.all_to_all(
        jnp.concatenate([real_twist, imag_twist], 0), "seq", split_axis=2, concat_axis=1, tiled=True
    )
    row_cos, row_sin = angle_table(part_count, row_order, row_order, 0, 0, 1.0)
    signal = (
        jnp.einsum("aj,kjbf->kabf", row_cos, by_column[:stack_size], precision=HIGHEST)
        - jnp.einsum("aj,kjbf->kabf", row_sin, by_column[stack_size:], precision=HIGHEST)
    ) / row_order
    returned = lax.all_to_all(signal, "seq", split_axis=1, concat_axis=2, tiled=True)
    return returned[:, 0]


def panel_local(inputs, gate_branch, short_taps, filters, w_out, cotangent):
    forward_fn, inverse_fn = (panel_forward, panel_inverse)
    tap_count = short_taps.shape[0]
    row_count = inputs.shape[0]
    left_tail = from_behind(inputs[row_count - (tap_count - 1) :], "seq", 1)
    extended = jnp.concatenate([left_tail, inputs], 0).astype(jnp.float32)
    mixed = jnp.zeros((row_count, inputs.shape[1]), jnp.float32)
    for tap_index in range(tap_count):
        start_row = tap_count - 1 - tap_index
        mixed = mixed + short_taps[tap_index] * extended[start_row : start_row + row_count]
    spec_real, spec_imag = forward_fn(jnp.stack([mixed, filters], 0))
    mixed_real, filter_real = (spec_real[0], spec_real[1])
    mixed_imag, filter_imag = (spec_imag[0], spec_imag[1])
    prod_real = mixed_real * filter_real - mixed_imag * filter_imag
    prod_imag = mixed_real * filter_imag + mixed_imag * filter_real
    convolved = inverse_fn(prod_real[None], prod_imag[None])[0]
    gate_wide = gate_branch.astype(jnp.float32)
    gated = (gate_wide * convolved).astype(jnp.bfloat16)
    out_terms = jnp.dot(gated, w_out, preferred_element_type=jnp.float32)
    output = lax.psum_scatter(out_terms, "chan", scatter_dimension=1, tiled=True).astype(
        jnp.bfloat16
    )
    full_cot = lax.all_gather(cotangent, "chan", axis=1, tiled=True)
    grad_gated = lax.dot_general(
        full_cot, w_out, (((1,), (1,)), ((), ())), preferred_element_type=jnp.float32
    )
    grad_gate = (grad_gated * convolved).astype(jnp.bfloat16)
    grad_conv = grad_gated * gate_wide
    grad_real, grad_imag = forward_fn(grad_conv[None])
    grad_real = grad_real[0]
    grad_imag = grad_imag[0]
    back_real = jnp.stack(
        [
            filter_real * grad_real + filter_imag * grad_imag,
            mixed_real * grad_real + mixed_imag * grad_imag,
        ],
        0,
    )
    back_imag = jnp.stack(
        [
            filter_real * grad_imag - filter_imag * grad_real,
            mixed_real * grad_imag - mixed_imag * grad_real,
        ],
        0,
    )
    gradients = inverse_fn(back_real, back_imag)
    grad_mixed = gradients[0]
    grad_filters = gradients[1]
    right_head = from_behind(grad_mixed[: tap_count - 1], "seq", -1)
    grad_ext = jnp.concatenate([grad_mixed, right_head], 0)
    grad_wide = jnp.zeros_like(grad_mixed)
    tap_rows = []
    for tap_index in range(tap_count):
        start_row = tap_count - 1 - tap_index
        grad_wide = grad_wide + short_taps[tap_index] * grad_ext[tap_index : tap_index + row_count]
        tap_rows.append(jnp.sum(extended[start_row : start_row + row_count] * grad_mixed, axis=0))
    grad_inputs = grad_wide.astype(jnp.bfloat16)
    grad_taps = lax.psum(jnp.stack(tap_rows, 0), "seq")
    weight_terms = lax.dot_general(
        gated, full_cot, (((0,), (0,)), ((), ())), preferred_element_type=jnp.float32
    )
    grad_wout = lax.psum_scatter(weight_terms, "seq", scatter_dimension=1, tiled=True)
    return (output, grad_inputs, grad_gate, grad_filters, grad_taps, grad_wout)


DENSE_TOKENS = 2048


def split_table(table):
    high = table.astype(jnp.bfloat16)
    low = (table - high.astype(np.float64)).astype(jnp.bfloat16)
    return (high, low)


def dense_tables(tokens):
    freq = np.arange(tokens, dtype=np.int64)[:, None]
    time = np.arange(tokens, dtype=np.int64)[None, :]
    angles = ((2 * freq + 1) * time % (4 * tokens)) * (2.0 * np.pi / (4 * tokens))
    forward = np.concatenate([np.cos(angles), -np.sin(angles)], 0)
    inverse = forward.T / tokens
    return (split_table(forward), split_table(inverse))


LANES = 128
HALF = 64
TILE = 256
DOT_TILE = 1024
BF16 = jnp.bfloat16
F32 = jnp.float32


def left_half(shape):
    return lax.broadcasted_iota(jnp.int32, shape, 1) < HALF


def turned(value):
    return pltpu.roll(value, HALF, 1)


def split_value(value):
    high = value.astype(BF16)
    return (high, (value - high.astype(F32)).astype(BF16))


def packed_split(value):
    high = value.astype(BF16).astype(F32)
    return jnp.where(left_half(value.shape), high, value - high).astype(BF16)


def tiles(count, body, size=TILE):
    def step(index, carry):
        body(pl.ds(pl.multiple_of(index * size, size), size))
        return carry

    lax.fori_loop(0, count // size, step, 0)


def product(left, right):
    return jnp.dot(left, right, preferred_element_type=F32)


def wide_transform(high, low, value, result):
    def body(rows):
        first = product(high[rows, :], value[...])
        second = product(low[rows, :], value[:, :LANES])
        result[rows, :] = first[:, :LANES] + first[:, LANES:] + second

    tiles(result.shape[0], body, DOT_TILE)


def half_transform(high, low, value, result):
    def body(rows):
        total = product(high[rows, :], value[...]) + product(low[rows, :], value[...])
        result[rows, :] = total + turned(total)

    tiles(result.shape[0], body, DOT_TILE)


def moved(value, steps):
    if steps == 0:
        return value
    count = value.shape[0]
    row = lax.broadcasted_iota(jnp.int32, value.shape, 0)
    keep = (row >= steps) if steps > 0 else (row < count + steps)
    return jnp.where(keep, pltpu.roll(value, steps % count, 0), 0.0)


def block_kernel(
    inputs, gate, taps, filters, w_out_hbm, cot, fwd_high_hbm, fwd_low_hbm, inv_high_hbm, inv_low_hbm,
    output, grad_inputs, grad_gate, grad_filters, grad_taps, grad_wout,
    w_out, fwd_high, fwd_low, inv_high, inv_low, cot_all, cot_send, cot_cols, first_send, first_got,
    second_send, second_got, gated_all, own_got, third_send, third_got, gate_send, gate_got,
    taps_send, taps_got, part_send, part_got, wide_short, half_short, half_long, wide_long,
    spec, grad_spec, signal, mixing, table_sems, send_sems, recv_sems, chan_send_sems, chan_recv_sems,
):
    parts, rows = first_got.shape[0], first_got.shape[1]
    chans, cols = cot_all.shape[0], inputs.shape[1]
    tokens = parts * rows
    tap_count = taps.shape[0]
    me = lax.axis_index("seq")
    mine = lax.axis_index("chan")

    tables = [
        pltpu.make_async_copy(source, target, table_sems.at[index])
        for index, (source, target) in enumerate(
            [
                (w_out_hbm, w_out), (fwd_high_hbm, fwd_high), (fwd_low_hbm, fwd_low),
                (inv_high_hbm, inv_high), (inv_low_hbm, inv_low),
            ]
        )
    ]
    for table in tables:
        table.start()

    barrier = pltpu.get_barrier_semaphore()
    for step in range(1, parts):
        pl.semaphore_signal(
            barrier, inc=1, device_id=(lax.rem(me + step, parts), mine),
            device_id_type=pl.DeviceIdType.MESH,
        )
    for step in range(1, chans):
        pl.semaphore_signal(
            barrier, inc=1, device_id=(me, lax.rem(mine + step, chans)),
            device_id_type=pl.DeviceIdType.MESH,
        )
    pl.semaphore_wait(barrier, parts + chans - 2)

    def to_seq(kind, step, source, target):
        return pltpu.make_async_remote_copy(
            src_ref=source, dst_ref=target,
            send_sem=send_sems.at[kind, step], recv_sem=recv_sems.at[kind, step],
            device_id=(lax.rem(me + step, parts), mine), device_id_type=pl.DeviceIdType.MESH,
        )

    def to_chan(kind, step, source, target):
        return pltpu.make_async_remote_copy(
            src_ref=source, dst_ref=target,
            send_sem=chan_send_sems.at[kind, step], recv_sem=chan_recv_sems.at[kind, step],
            device_id=(me, lax.rem(mine + step, chans)), device_id_type=pl.DeviceIdType.MESH,
        )

    def launch(copies):
        for copy in copies:
            copy.start()
        return copies

    def arrive(copies):
        for copy in copies:
            copy.wait_recv()

    def exchange(kind, sent, got):
        copies = launch(
            [
                to_seq(kind, step, sent.at[lax.rem(me + step, parts)], got.at[me])
                for step in range(1, parts)
            ]
        )
        got[pl.ds(me, 1)] = sent[pl.ds(me, 1)]
        return copies

    def pack(left, right, target):
        for pair in range(parts // 2):
            span = slice(pair * LANES, (pair + 1) * LANES)
            a, b = (left[:, span].astype(F32), right[:, span].astype(F32))
            low = left_half(a.shape)
            target[2 * pair] = jnp.where(low, a, turned(b)).astype(BF16)
            target[2 * pair + 1] = jnp.where(low, turned(a), b).astype(BF16)

    cot_copies = launch([to_chan(0, step, cot, cot_all.at[mine]) for step in range(1, chans)])
    cot_all[pl.ds(mine, 1)] = cot[...][None]
    pack(inputs, filters, first_send)
    first_copies = exchange(0, first_send, first_got)

    own_taps = taps[:, pl.ds(pl.multiple_of(lax.div(me, 2) * LANES, LANES), LANES)]
    odd = jnp.full(own_taps.shape, lax.rem(me, 2), jnp.int32) == 1
    own_taps = jnp.where(odd, turned(own_taps), own_taps)
    tap_ids = lax.broadcasted_iota(jnp.int32, own_taps.shape, 0)
    mixing[...] = jnp.where(left_half(own_taps.shape), own_taps, (tap_ids == 0).astype(F32))

    arrive(first_copies)
    packed = first_got[...].reshape(tokens, LANES).astype(F32)
    mixed = packed * mixing[0:1, :]
    for tap in range(1, tap_count):
        mixed = mixed + mixing[tap : tap + 1, :] * moved(packed, tap)
    high, low = split_value(mixed)
    wide_short[:, :LANES] = high
    wide_short[:, LANES:] = low
    tables[1].wait()
    tables[2].wait()
    wide_transform(fwd_high, fwd_low, wide_short, spec)

    arrive(cot_copies)
    tables[0].wait()
    grad_gated = jnp.zeros((rows, cols), F32)
    for chan in range(chans):
        grad_gated = grad_gated + lax.dot_general(
            cot_all[chan], w_out[:, chan * cols : (chan + 1) * cols],
            (((1,), (1,)), ((), ())), preferred_element_type=F32,
        )
    pack(gate, grad_gated, second_send)
    second_copies = exchange(1, second_send, second_got)
    share = chans * cols // parts
    quarter_rows = rows // chans
    quarter = pl.ds(pl.multiple_of(mine * quarter_rows, quarter_rows), quarter_rows)
    for part in range(parts):
        chan, start = divmod(part * share, cols)
        cot_send[part] = cot_all[chan, quarter, start : start + share]
    cot_col_copies = launch(
        [
            to_seq(
                2, step, cot_send.at[lax.rem(me + step, parts)], cot_cols.at[me, quarter]
            )
            for step in range(1, parts)
        ]
    )
    cot_cols[pl.ds(me, 1), quarter] = cot_send[pl.ds(me, 1)]

    def multiply(rows_at):
        other = pl.ds(pl.multiple_of(rows_at.start + tokens, TILE), TILE)
        real, imag = (spec[rows_at, :], spec[other, :])
        real_turned, imag_turned = (turned(real), turned(imag))
        half_long[rows_at, :] = packed_split(real * real_turned - imag * imag_turned)
        half_long[other, :] = packed_split(real * imag_turned + imag * real_turned)

    tiles(tokens, multiply)
    tables[3].wait()
    tables[4].wait()
    half_transform(inv_high, inv_low, half_long, signal)

    arrive(cot_col_copies)
    cot_row_copies = launch(
        [
            to_chan(2, step, cot_cols.at[:, quarter], cot_cols.at[:, quarter])
            for step in range(1, chans)
        ]
    )
    arrive(second_copies)
    for part in range(parts):
        span = slice(part * rows, (part + 1) * rows)
        branch = second_got[part].astype(F32)
        scaled = branch * signal[span, :]
        gated_all[pl.ds(me, 1), :, span] = scaled.T[:HALF].astype(BF16)[None]
        gate_send[part] = jnp.where(
            left_half((rows // 2, LANES)), turned(scaled[: rows // 2]), scaled[rows // 2 :]
        ).astype(BF16)
        half_short[span, :] = packed_split(branch * turned(branch))

    own_copies = launch(
        [
            to_seq(
                7, step,
                gated_all.at[
                    me, :, pl.ds(pl.multiple_of(lax.rem(me + step, parts) * rows, rows), rows)
                ],
                own_got.at[me],
            )
            for step in range(1, parts)
        ]
    )
    here = pl.ds(pl.multiple_of(me * rows, rows), rows)
    own_got[pl.ds(me, 1)] = gated_all[pl.ds(me, 1), :, here]
    line = [
        launch(
            [
                to_seq(kind, step, gated_all.at[me, span], gated_all.at[me, span])
                for step in range(2, parts, 2)
            ]
        )
        for kind, span in ((3, slice(0, HALF // 2)), (9, slice(HALF // 2, HALF)))
    ]
    partner = me + 1 - 2 * lax.rem(me, 2)

    def hand_on(kind, step, span):
        source = lax.rem(me + parts - step, parts)
        return pltpu.make_async_remote_copy(
            src_ref=gated_all.at[source, span], dst_ref=gated_all.at[source, span],
            send_sem=send_sems.at[kind, step], recv_sem=recv_sems.at[kind, step],
            device_id=(partner, mine), device_id_type=pl.DeviceIdType.MESH,
        )

    handed = launch([hand_on(8, 0, slice(0, HALF))])

    half_transform(fwd_high, fwd_low, half_short, grad_spec)

    arrive(own_copies)
    own_gated = own_got[...].astype(F32).reshape(parts * HALF, rows).T.astype(BF16)
    for chan in range(chans):
        part_send[chan] = product(own_gated, w_out[:, chan * cols : (chan + 1) * cols]).astype(BF16)
    part_copies = launch(
        [
            to_chan(1, step, part_send.at[lax.rem(mine + step, chans)], part_got.at[mine])
            for step in range(1, chans)
        ]
    )
    part_got[pl.ds(mine, 1)] = part_send[pl.ds(mine, 1)]

    for step, copy in zip(range(2, parts, 2), line[0]):
        copy.wait_recv()
        handed += launch([hand_on(8, step, slice(0, HALF // 2))])
    gate_copies = exchange(4, gate_send, gate_got)

    def back(rows_at):
        other = pl.ds(pl.multiple_of(rows_at.start + tokens, TILE), TILE)
        real, imag = (turned(spec[rows_at, :]), turned(spec[other, :]))
        grad_real, grad_imag = (grad_spec[rows_at, :], grad_spec[other, :])
        high, low = split_value(real * grad_real + imag * grad_imag)
        wide_long[rows_at, :LANES] = high
        wide_long[rows_at, LANES:] = low
        high, low = split_value(real * grad_imag - imag * grad_real)
        wide_long[other, :LANES] = high
        wide_long[other, LANES:] = low

    tiles(tokens, back)
    wide_transform(inv_high, inv_low, wide_long, signal)
    for step, copy in zip(range(2, parts, 2), line[1]):
        copy.wait_recv()
        handed += launch([hand_on(10, step, slice(HALF // 2, HALF))])
    grads = signal[...]
    mixed_back = grads * mixing[0:1, :]
    packed = first_got[...].reshape(tokens, LANES).astype(F32)
    taps_send[...] = jnp.zeros_like(taps_send)
    for tap in range(tap_count):
        if tap:
            mixed_back = mixed_back + mixing[tap : tap + 1, :] * moved(grads, -tap)
        taps_send[tap : tap + 1, :] = jnp.sum(
            moved(packed, tap) * grads, axis=0, keepdims=True
        )
    third_send[...] = mixed_back.astype(BF16).reshape(parts, rows, LANES)
    third_copies = exchange(5, third_send, third_got)
    taps_copies = launch(
        [to_seq(6, step, taps_send, taps_got.at[me]) for step in range(1, parts)]
    )
    taps_got[pl.ds(me, 1)] = taps_send[...][None]

    arrive(cot_row_copies)
    arrive(handed)
    grad_wout[...] = product(
        gated_all[...].reshape(parts * HALF, tokens), cot_cols[...].reshape(tokens, share)
    )
    arrive(gate_copies)
    arrive(third_copies)
    arrive(taps_copies)
    for pair in range(parts // 2):
        span = slice(pair * LANES, (pair + 1) * LANES)
        a, b = (third_got[2 * pair].astype(F32), third_got[2 * pair + 1].astype(F32))
        low = left_half(a.shape)
        grad_inputs[:, span] = jnp.where(low, a, turned(b)).astype(BF16)
        grad_filters[:, span] = jnp.where(low, turned(a), b)
        a, b = (gate_got[2 * pair].astype(F32), gate_got[2 * pair + 1].astype(F32))
        low = left_half(a.shape)
        grad_gate[: rows // 2, span] = jnp.where(low, a, turned(b)).astype(BF16)
        grad_gate[rows // 2 :, span] = jnp.where(low, turned(a), b).astype(BF16)
        a, b = (taps_got[2 * pair], taps_got[2 * pair + 1])
        grad_taps[:, span] = jnp.where(left_half(a.shape), a, turned(b))[:tap_count]

    arrive(part_copies)
    total = part_got[0].astype(F32)
    for chan in range(1, chans):
        total = total + part_got[chan].astype(F32)
    output[...] = total.astype(BF16)
    for copies in (
        cot_copies, first_copies, second_copies, cot_col_copies, cot_row_copies, own_copies, *line,
        handed, gate_copies, third_copies, taps_copies, part_copies,
    ):
        for copy in copies:
            copy.wait_send()


def store_kernel(*refs):
    count = len(refs) // 2
    for source, target in zip(refs[:count], refs[count:]):
        target[...] = source[...]


def dense_local(inputs, gate_branch, short_taps, filters, w_out, cotangent):
    parts = lax.axis_size("seq")
    chans = lax.axis_size("chan")
    rows, cols = inputs.shape
    tokens = rows * parts
    share = cols * chans // parts
    tap_rows = 8
    (fwd_high, fwd_low), (inv_high, inv_low) = dense_tables(tokens)
    vmem = pl.BlockSpec(memory_space=pltpu.VMEM)
    hbm = pl.BlockSpec(memory_space=pl.ANY)
    shape = jax.ShapeDtypeStruct
    results = pl.pallas_call(
        block_kernel,
        out_shape=(
            shape((rows, cols), BF16), shape((rows, cols), BF16), shape((rows, cols), BF16),
            shape((rows, cols), F32), shape(short_taps.shape, F32), shape((cols, share), F32),
        ),
        in_specs=[vmem] * 4 + [hbm, vmem] + [hbm] * 4,
        out_specs=[vmem] * 6,
        scratch_shapes=[
            pltpu.VMEM(w_out.shape, BF16),
            pltpu.VMEM((2 * tokens, tokens), BF16), pltpu.VMEM((2 * tokens, tokens), BF16),
            pltpu.VMEM((tokens, 2 * tokens), BF16), pltpu.VMEM((tokens, 2 * tokens), BF16),
            pltpu.VMEM((chans, rows, cols), BF16),
            pltpu.VMEM((parts, rows // chans, share), BF16), pltpu.VMEM((parts, rows, share), BF16),
            pltpu.VMEM((parts, rows, LANES), BF16), pltpu.VMEM((parts, rows, LANES), BF16),
            pltpu.VMEM((parts, rows, LANES), BF16), pltpu.VMEM((parts, rows, LANES), BF16),
            pltpu.VMEM((parts, HALF, tokens), BF16), pltpu.VMEM((parts, HALF, rows), BF16),
            pltpu.VMEM((parts, rows, LANES), BF16), pltpu.VMEM((parts, rows, LANES), BF16),
            pltpu.VMEM((parts, rows // 2, LANES), BF16), pltpu.VMEM((parts, rows // 2, LANES), BF16),
            pltpu.VMEM((tap_rows, LANES), F32), pltpu.VMEM((parts, tap_rows, LANES), F32),
            pltpu.VMEM((chans, rows, cols), BF16), pltpu.VMEM((chans, rows, cols), BF16),
            pltpu.VMEM((tokens, 2 * LANES), BF16), pltpu.VMEM((tokens, LANES), BF16),
            pltpu.VMEM((2 * tokens, LANES), BF16), pltpu.VMEM((2 * tokens, 2 * LANES), BF16),
            pltpu.VMEM((2 * tokens, LANES), F32), pltpu.VMEM((2 * tokens, LANES), F32),
            pltpu.VMEM((tokens, LANES), F32), pltpu.VMEM((short_taps.shape[0], LANES), F32),
            pltpu.SemaphoreType.DMA((5,)),
            pltpu.SemaphoreType.DMA((11, parts)), pltpu.SemaphoreType.DMA((11, parts)),
            pltpu.SemaphoreType.DMA((3, chans)), pltpu.SemaphoreType.DMA((3, chans)),
        ],
        compiler_params=pltpu.CompilerParams(
            collective_id=0, has_side_effects=True, vmem_limit_bytes=56 * 1024 * 1024
        ),
    )(inputs, gate_branch, short_taps, filters, w_out, cotangent, fwd_high, fwd_low, inv_high, inv_low)
    count = len(results)
    return pl.pallas_call(
        store_kernel,
        out_shape=[shape(value.shape, value.dtype) for value in results],
        in_specs=[vmem] * count,
        out_specs=[vmem] * count,
    )(*results)


def local(inputs, *others):
    parts = lax.axis_size("seq")
    rows, cols = inputs.shape
    fits = rows * parts <= DENSE_TOKENS and rows % LANES == 0 and parts % 2 == 0
    fits = fits and cols == HALF * parts and rows % (16 * lax.axis_size("chan")) == 0
    return (dense_local if fits else panel_local)(inputs, *others)


def solution(mesh):
    in_specs = (
        P("seq", "chan"),
        P("seq", "chan"),
        P(None, "chan"),
        P("seq", "chan"),
        P("chan", None),
        P("seq", "chan"),
    )
    out_specs = (
        P("seq", "chan"),
        P("seq", "chan"),
        P("seq", "chan"),
        P("seq", "chan"),
        P(None, "chan"),
        P("chan", "seq"),
    )
    return jax.shard_map(local, mesh=mesh, in_specs=in_specs, out_specs=out_specs, check_vma=False)
```
